128 devices in a mesh: ctx: 16 (over z, y_hi, core), exp: 8 (over x, y_lo).
Axes of the slice: x: 4, y: 4 (y_hi: 2, y_lo: 2; y = y_hi * 2 + y_lo), z: 4, core: 2. Of those that a mesh axis runs over, the one named last changes fastest.
Arguments:
- tokens: bfloat16 [16384, 2048], P(('ctx', 'exp')), may hold values from -12 to 12
- ln1_gain: float32 [2048], replicated, may hold values from 0.5 to 2
- w_query: bfloat16 [2048, 2048], P(None, 'exp')
- key_weight: bfloat16 [2048, 256], replicated
- value_weight: bfloat16 [2048, 256], replicated, may hold values from -0.125 to 0.125
- q_gain: float32 [128], replicated, may hold values from 0.5 to 5.5
- k_gain: float32 [128], replicated, may hold values from 0.5 to 5.5
- w_out: bfloat16 [2048, 2048], P('exp'), may hold values from -0.125 to 0.125
- ln2_gain: float32 [2048], replicated, may hold values from 0.5 to 2
- expert_ids: int32 [16384, 8], P(('ctx', 'exp')), may hold values from 0 to 127, all different within a row; in each aligned block of 128 rows (0 to 127, 128 to 255, ...) at most 12 rows name the same one
- route_weights: int32 [16384, 8], P(('ctx', 'exp')), may hold values from 1 to 255
- w_gate: bfloat16 [128, 2048, 768], P(('ctx', 'exp')), may hold values from -0.125 to 0.125
- w_up: bfloat16 [128, 2048, 768], P(('ctx', 'exp')), may hold values from -0.125 to 0.125
- w_down: bfloat16 [128, 768, 2048], P(('ctx', 'exp')), may hold values from -0.21875 to 0.21875
Outputs:
- layer_out: bfloat16 [16384, 2048], P(('ctx', 'exp'))
The draws below stay inside these ranges and needn't reach their ends.
Inputs may be any that keep to these rules, and one draw needn't show every extreme that they name: `expert_ids`: each token names 8 different experts; among the 128 rows of one device no expert is named by more than 12 rows. `route_weights`: a choice weighs the value divided by 1024.
All inputs are finite; a program needn't handle non-finite values.
Results may differ from the reference program's by a relative error of at most 0.02.
The reference program's roundings to bfloat16 on the way count: a program that leaves them out, or rounds other values in their place, can miss the bound.
Values may be sent and summed in bfloat16 or wider, within the bound.
A program may use at most 128 MiB of HBM per device.

```python
import math
import jax
import jax.numpy as jnp
import numpy as np
from jax import lax

MODEL_WIDTH = 2048
HEAD_SIZE = 128
QUERY_HEADS = 16
KEY_VALUE_HEADS = 2
FF = 768
TOP = 8
TOK_DEV = 128
SEQUENCE_TOKENS = 16384
EXPERTS = 128
CAP = 12


def draw_tokens(key, part):
    raw_key, scale_key = jax.random.split(key, 2)
    scales = jnp.exp(jax.random.uniform(scale_key, (SEQUENCE_TOKENS, 1), jnp.float32, jnp.log(0.5), jnp.log(2.0)))
    values_raw = jnp.clip(jax.random.normal(raw_key, (SEQUENCE_TOKENS, MODEL_WIDTH), jnp.float32), -6.0, 6.0)
    return (values_raw * scales).astype(jnp.bfloat16)


def key_matrix(key):
    return jax.random.normal(jax.random.fold_in(key, 7), (MODEL_WIDTH, KEY_VALUE_HEADS * HEAD_SIZE), jnp.float32) * MODEL_WIDTH ** (-0.5)


def draw_key_weight(key, part):
    return key_matrix(key).astype(jnp.bfloat16)


def draw_w_query(key, part):
    weight_matrix = jax.random.normal(jax.random.fold_in(key, 11), (MODEL_WIDTH, QUERY_HEADS * HEAD_SIZE), jnp.float32) * MODEL_WIDTH ** (-0.5)
    return weight_matrix.astype(jnp.bfloat16)


def gain_vector(key, salt_value):
    folded = jax.random.fold_in(key, salt_value)
    return jnp.exp(jax.random.uniform(folded, (HEAD_SIZE,), jnp.float32, jnp.log(0.5), jnp.log(2.0)))


def draw_q_gain(key, part):
    return gain_vector(key, 3)


def draw_k_gain(key, part):
    return gain_vector(key, 5)


def with_ends(entries, stream_key, smallest, top_value):
    index_at = [jax.random.randint(jax.random.fold_in(stream_key, axis), (), 0, length) for axis, length in enumerate(entries.shape)]
    main_axis = entries.shape.index(max(entries.shape))
    neighbour = index_at[:main_axis] + [(index_at[main_axis] + 1) % entries.shape[main_axis]] + index_at[main_axis + 1:]
    return entries.at[tuple(index_at)].set(smallest).at[tuple(neighbour)].set(top_value)


def shard_levels(own_key, dims, cuts, low, largest):
    factor_of = 1.0
    for axis_at, blocks in cuts:
        steps = jax.random.uniform(jax.random.fold_in(jax.random.fold_in(own_key, 6), axis_at), (blocks,), jnp.float32, low / len(cuts), largest / len(cuts))
        factor_of = factor_of * jnp.repeat(jnp.exp(steps), dims[axis_at] // blocks).reshape((-1,) + (1,) * (len(dims) - 1 - axis_at))
    return factor_of


def assign_block(rng, own, number, rows, count, top, limit, skew):
    ranking = jax.random.permutation(rng, count)
    heavy_load, ordinary = load_shares(count, rows * top, limit, skew, True), load_shares(count, rows * top, limit, skew, False)
    places = jnp.arange(count)

    def named(tallies, rotation):
        used = int((tallies > 0).sum())
        fixed = max(1, used // 4)
        shifted = fixed + (places - fixed + rotation * (used - fixed)) % max(1, count - fixed)
        return jnp.zeros((count,), jnp.int32).at[ranking[jnp.where(places < fixed, places, shifted)]].set(jnp.asarray(tallies, jnp.int32))

    tallies = jnp.where(number % 4 == 0, named(heavy_load, number // 4), named(ordinary, number - number // 4 - 1))
    mixed = jax.random.permutation(jax.random.fold_in(own, 3), count)
    source_of, taker = mixed[0:count // 2 * 2:2], mixed[1:count // 2 * 2:2]
    slack = jnp.minimum(tallies[source_of] - 1, limit - tallies[taker]) // 2
    slack = jnp.where((source_of == ranking[0]) | (taker == ranking[0]) | (tallies[taker] == 0), 0, jnp.maximum(slack, 0))
    shifted = jax.random.randint(jax.random.fold_in(own, 4), (count // 2,), 0, 1 << 20) % (slack + 1)
    tallies = tallies.at[source_of].add(-shifted).at[taker].add(shifted)
    items = jnp.searchsorted(jnp.cumsum(tallies), jnp.arange(rows * top), side="right").astype(jnp.int32)
    listing = items.reshape(top, rows).T
    listing = listing[jax.random.permutation(jax.random.fold_in(own, 1), rows)]
    rotation = jax.random.randint(jax.random.fold_in(own, 2), (rows, 1), 0, top)
    return jnp.take_along_axis(listing, (jnp.arange(top)[None, :] + rotation) % top, axis=1)


def load_shares(amount, total, bound, slope, full):
    weights = [(1 << 20) // math.isqrt(rank ** slope) + 1 for rank in range(1, amount + 1)]
    largest = bound if full else min(bound, max(-(-total // amount), total * weights[0] // sum(weights)))
    least = 1 if total - largest >= amount - 1 else 0
    counts, rest = [largest] + [least] * (amount - 1), total - largest - least * (amount - 1)
    while rest > 0:
        candidates = [i for i in range(1, amount) if counts[i] < largest] or [i for i in range(1, amount) if counts[i] < bound]
        mass, budget = sum([weights[i] for i in candidates]), rest
        for i in candidates:
            addition = min(bound - counts[i], max(1, budget * weights[i] // mass), rest)
            counts[i] = counts[i] + addition
            rest = rest - addition
    return np.array(counts)


def bell_draw(rng, shape, scale, most, cuts=(), held_as=jnp.bfloat16):
    array = jax.random.normal(rng, shape, jnp.float32) * scale
    if len(cuts) > 0:
        array = shard_levels(rng, shape, cuts, -0.22, 0.18) * array
    return jnp.clip(array, min=-most, max=most).astype(held_as)


def setup_inputs(seed: int = 0) -> dict:
    splits = jax.random.split(jax.random.key(seed), 15)
    tokens = draw_tokens(jax.random.fold_in(splits[14], 71), 0)
    ln1_gain = jnp.clip(jnp.exp(jax.random.uniform(splits[1], (MODEL_WIDTH,), jnp.float32, math.log(0.5), math.log(2.0))), 0.5, 2.0)
    w_query = draw_w_query(jax.random.fold_in(splits[14], 71), 0)
    key_weight = draw_key_weight(jax.random.fold_in(splits[14], 71), 0)
    value_weight = bell_draw(splits[4], (MODEL_WIDTH, KEY_VALUE_HEADS * HEAD_SIZE), MODEL_WIDTH ** -0.5, 0.125)
    q_gain = draw_q_gain(jax.random.fold_in(splits[14], 71), 0)
    k_gain = draw_k_gain(jax.random.fold_in(splits[14], 71), 0)
    w_out = bell_draw(splits[7], (QUERY_HEADS * HEAD_SIZE, MODEL_WIDTH), (QUERY_HEADS * HEAD_SIZE) ** -0.5, 0.125, ((0, 8),))
    ln2_gain = jnp.clip(jnp.exp(jax.random.uniform(splits[8], (MODEL_WIDTH,), jnp.float32, math.log(0.5), math.log(2.0))), 0.5, 2.0)
    expert_ids_keys = jax.random.split(jax.random.fold_in(splits[9], 1), SEQUENCE_TOKENS // TOK_DEV)
    expert_ids_turns = jax.random.permutation(jax.random.fold_in(splits[9], 3), SEQUENCE_TOKENS // TOK_DEV)
    expert_ids = jax.vmap(lambda own, number: assign_block(jax.random.fold_in(splits[9], 2), own, number, TOK_DEV, EXPERTS, TOP, CAP, 2))(expert_ids_keys, expert_ids_turns).reshape((SEQUENCE_TOKENS, TOP))
    route_weights = with_ends(jax.random.randint(splits[10], (SEQUENCE_TOKENS, TOP), 1, 256), jax.random.fold_in(splits[10], 1), 1, 255).astype(jnp.int32)
    w_gate = bell_draw(splits[11], (EXPERTS, MODEL_WIDTH, FF), MODEL_WIDTH ** -0.5, 0.125, ((0, 128),))
    w_up = bell_draw(splits[12], (EXPERTS, MODEL_WIDTH, FF), MODEL_WIDTH ** -0.5, 0.125, ((0, 128),))
    w_down = bell_draw(splits[13], (EXPERTS, FF, MODEL_WIDTH), FF ** -0.5, 0.21875, ((0, 128),))
    return {"tokens": tokens, "ln1_gain": ln1_gain, "w_query": w_query, "key_weight": key_weight, "value_weight": value_weight, "q_gain": q_gain, "k_gain": k_gain, "w_out": w_out, "ln2_gain": ln2_gain, "expert_ids": expert_ids, "route_weights": route_weights, "w_gate": w_gate, "w_up": w_up, "w_down": w_down}


eps_value = 1e-06
theta_value = 1000000.0

def rms_scale(value_states, norm_gain):
    return value_states * lax.rsqrt(lax.optimization_barrier(jnp.mean(value_states * value_states, axis=-1, keepdims=True)) + eps_value) * norm_gain

def rotate(value_states, positions):
    half_size = value_states.shape[-1] // 2
    frequency = theta_value ** (-2.0 * jnp.arange(half_size, dtype=jnp.float32) / value_states.shape[-1])
    angles = positions.astype(jnp.float32)[:, None] * frequency[None, :]
    cosine = jnp.cos(angles)
    sine_part = jnp.sin(angles)
    leading = value_states[..., :half_size]
    second = value_states[..., half_size:]
    return jnp.concatenate([leading * cosine - second * sine_part, second * cosine + leading * sine_part], axis=-1)

def reference(tokens, ln1_gain, w_query, key_weight, value_weight, q_gain, k_gain, w_out, ln2_gain, expert_ids, route_weights, w_gate, w_up, w_down):
    group_width = QUERY_HEADS // KEY_VALUE_HEADS
    inputs32 = tokens.astype(jnp.float32)
    normed_input = rms_scale(inputs32, ln1_gain).astype(jnp.bfloat16)
    positions = jnp.arange(SEQUENCE_TOKENS).astype(jnp.int32)
    query_all = jnp.dot(normed_input, w_query, preferred_element_type=jnp.float32).reshape(SEQUENCE_TOKENS, QUERY_HEADS, HEAD_SIZE).transpose(1, 0, 2)
    queries = rotate(rms_scale(query_all, q_gain), positions).astype(jnp.bfloat16)
    every_key = jnp.dot(normed_input, key_weight, preferred_element_type=jnp.float32).reshape(SEQUENCE_TOKENS, KEY_VALUE_HEADS, HEAD_SIZE).transpose(1, 0, 2)
    keys = rotate(rms_scale(every_key, k_gain), positions).astype(jnp.bfloat16)
    value_states = jnp.dot(normed_input, value_weight, preferred_element_type=jnp.float32).astype(jnp.bfloat16)
    value_states = value_states.reshape(SEQUENCE_TOKENS, KEY_VALUE_HEADS, HEAD_SIZE).transpose(1, 0, 2)
    query_block = min(SEQUENCE_TOKENS, 1024)
    block_count = SEQUENCE_TOKENS // query_block
    scale_factor = HEAD_SIZE ** (-0.5)

    def one_head(head_index):
        head_queries = queries[head_index].astype(jnp.float32)
        head_keys = keys[head_index // group_width].astype(jnp.float32)
        head_values = value_states[head_index // group_width].astype(jnp.float32)

        def one_block(block_index):
            first_row = (block_index * query_block).astype(jnp.int32)
            query_rows = lax.dynamic_slice_in_dim(head_queries, first_row, query_block, 0)
            scores = jnp.dot(query_rows, head_keys.T, precision=lax.Precision.HIGHEST) * scale_factor
            query_pos = first_row + jnp.arange(query_block).astype(jnp.int32)
            visible = positions[None, :] <= query_pos[:, None]
            scores = jnp.where(visible, scores, -jnp.inf)
            row_max = lax.optimization_barrier(jnp.max(scores, axis=1, keepdims=True))
            weights = jnp.exp(scores - row_max)
            row_sum = lax.optimization_barrier(jnp.sum(weights, axis=1, keepdims=True))
            rounded = lax.optimization_barrier(weights.astype(jnp.bfloat16)).astype(jnp.float32)
            mixed = jnp.dot(rounded, head_values, precision=lax.Precision.HIGHEST)
            return (mixed / row_sum).astype(jnp.bfloat16)
        return lax.map(one_block, jnp.arange(block_count)).reshape(SEQUENCE_TOKENS, HEAD_SIZE)
    attended = lax.map(one_head, jnp.arange(QUERY_HEADS))
    attended = attended.transpose(1, 0, 2).reshape(SEQUENCE_TOKENS, QUERY_HEADS * HEAD_SIZE)
    attention = jnp.dot(attended, w_out, preferred_element_type=jnp.float32)
    residual = (inputs32 + attention).astype(jnp.bfloat16)
    normed2 = rms_scale(residual.astype(jnp.float32), ln2_gain).astype(jnp.bfloat16)
    slots_total = SEQUENCE_TOKENS // TOK_DEV * CAP
    flat_ids = expert_ids.reshape(-1)
    flat_tokens = (jnp.arange(SEQUENCE_TOKENS * TOP) // TOP).astype(jnp.int32)
    flat_weights = route_weights.reshape(-1).astype(jnp.float32) / 1024.0
    chosen = (flat_ids[:, None] == jnp.arange(EXPERTS)[None, :]).astype(jnp.int32)
    rank_table = jnp.cumsum(chosen, axis=0) - chosen
    slot_index = lax.optimization_barrier(jnp.sum(rank_table * chosen, axis=1))
    table_rows = jnp.zeros((EXPERTS, slots_total), jnp.int32).at[flat_ids, slot_index].set(flat_tokens)
    table_weights = jnp.zeros((EXPERTS, slots_total), jnp.float32).at[flat_ids, slot_index].set(flat_weights)

    def add_expert(mixture, expert_inputs):
        rows_index, row_weights, gate_matrix, up_matrix, down_matrix = expert_inputs
        gathered = normed2[rows_index]
        gate_act = jnp.dot(gathered, gate_matrix, preferred_element_type=jnp.float32)
        up_act = jnp.dot(gathered, up_matrix, preferred_element_type=jnp.float32)
        hidden = (jax.nn.silu(gate_act) * up_act).astype(jnp.bfloat16)
        produced = jnp.dot(hidden, down_matrix, preferred_element_type=jnp.float32).astype(jnp.bfloat16)
        return (mixture.at[rows_index].add(row_weights[:, None] * produced.astype(jnp.float32)), None)
    mixture, unused = lax.scan(add_expert, jnp.zeros((SEQUENCE_TOKENS, MODEL_WIDTH), jnp.float32), (table_rows, table_weights, w_gate, w_up, w_down))
    return (residual.astype(jnp.float32) + mixture).astype(jnp.bfloat16)
```

```python
import functools

import jax
import jax.numpy as jnp
from jax import lax
from jax.experimental import pallas as pl
from jax.experimental.pallas import tpu as pltpu
from jax.sharding import PartitionSpec as P

HEAD = 128
KV_HEADS = 2
TOP = 8
CAP = 12
ROWS = 128
WIDTH = 2048
FF = 768
DEVS = 128
EPS = 1e-06
THETA = 1000000.0
CHUNK = 1024
BOTH = ("ctx", "exp")
MESH = pl.DeviceIdType.MESH


def rms_scale(v, gain):
    return v * lax.rsqrt(jnp.mean(v * v, axis=-1, keepdims=True) + EPS) * gain


def rope_tables(first):
    half = HEAD // 2
    frequency = THETA ** (-2.0 * jnp.arange(half, dtype=jnp.float32) / HEAD)
    positions = (first + jnp.arange(ROWS)).astype(jnp.float32)
    angles = positions[:, None] * frequency[None, :]
    return jnp.cos(angles), jnp.sin(angles)


def rotate(v, cos, sin):
    half = HEAD // 2
    a, b = v[..., :half], v[..., half:]
    return jnp.concatenate([a * cos - b * sin, b * cos + a * sin], axis=-1)


def place():
    c, e = lax.axis_index("ctx"), lax.axis_index("exp")
    return e // 2, (c // 2) % 2 * 2 + e % 2, c // 4, c % 2


def ids(x, y, z, core):
    return ((z * 2 + y // 2) * 2 + core, x * 2 + y % 2)


def gather_kernel(own, buf, out_sem, x_sem, y_sem, z_sem, f_sem, own_sem):
    x, y, z, c = place()
    yh, yl = y // 2, y % 2
    near = [(lax.rem(x + dx, 4), lax.rem(c + dc, 2)) for dc in range(2) for dx in range(4)]
    ys = [lax.rem(y + d, 4) for d in range(1, 4)]
    zs = [lax.rem(z + d, 4) for d in range(1, 4)]

    barrier = pltpu.get_barrier_semaphore()
    peers = [ids(px, y, z, pc) for px, pc in near[1:]]
    peers += [ids(x, py, z, c) for py in ys] + [ids(x, y, pz, c) for pz in zs]
    for peer in peers:
        pl.semaphore_signal(barrier, inc=1, device_id=peer, device_id_type=MESH)
    pl.semaphore_wait(barrier, len(peers))

    sent = []

    def send(src, dst, slot, sem, peer):
        copy = pltpu.make_async_remote_copy(
            src_ref=src,
            dst_ref=dst,
            send_sem=out_sem.at[slot],
            recv_sem=sem,
            device_id=peer,
            device_id_type=MESH,
        )
        copy.start()
        sent.append(copy)
        return copy

    mine = pltpu.make_async_copy(own.at[x // 2, c], buf.at[c, z, yh, c, x, yl], own_sem)
    mine.start()
    first = []
    for i, (px, pc) in enumerate(near):
        if i:
            first.append(
                send(
                    own.at[px // 2, pc],
                    buf.at[pc, z, yh, c, x, yl],
                    i - 1,
                    x_sem.at[i - 1],
                    ids(px, y, z, pc),
                )
            )
    for copy in first:
        copy.wait_recv()
    mine.wait()

    low, high = pl.ds(0, 2), pl.ds(2, 2)
    every2, every4 = pl.ds(0, 2), pl.ds(0, 4)
    a1 = buf.at[c, z, yh, every2, low, yl]
    b1 = buf.at[c, z, yh, every2, high, yl]
    second_a = [send(a1, a1, 7 + i, y_sem.at[i], ids(x, ys[i], z, c)) for i in range(3)]
    second_b = [send(b1, b1, 10 + i, z_sem.at[i], ids(x, y, zs[i], c)) for i in range(3)]
    for copy in second_a + second_b:
        copy.wait_recv()

    a2 = buf.at[c, z, every2, every2, low, every2]
    b2 = buf.at[c, every4, yh, every2, high, yl]
    third_a = [send(a2, a2, 13 + i, z_sem.at[3 + i], ids(x, y, zs[i], c)) for i in range(3)]
    third_b = [send(b2, b2, 16 + i, y_sem.at[3 + i], ids(x, ys[i], z, c)) for i in range(3)]
    other = ids(x, y, z, 1 - c)
    handed = [send(a2, a2, 19, f_sem.at[0], other), send(b2, b2, 20, f_sem.at[1], other)]
    for i in range(3):
        third_a[i].wait_recv()
        part = buf.at[c, lax.rem(z + 3 - i, 4), every2, every2, low, every2]
        handed.append(send(part, part, 21 + i, f_sem.at[2 + i], other))
        third_b[i].wait_recv()
        py = lax.rem(y + 3 - i, 4)
        part = buf.at[c, every4, py // 2, every2, high, py % 2]
        handed.append(send(part, part, 24 + i, f_sem.at[5 + i], other))
    for copy in handed:
        copy.wait_recv()
    for copy in sent:
        copy.wait_send()


def gather_kv(own):
    return pl.pallas_call(
        gather_kernel,
        out_shape=jax.ShapeDtypeStruct((2, 4, 2, 2, 4, 2, ROWS, HEAD), jnp.bfloat16),
        in_specs=[pl.BlockSpec(memory_space=pl.ANY)],
        out_specs=pl.BlockSpec(memory_space=pl.ANY),
        scratch_shapes=[
            pltpu.SemaphoreType.DMA((27,)),
            pltpu.SemaphoreType.DMA((7,)),
            pltpu.SemaphoreType.DMA((6,)),
            pltpu.SemaphoreType.DMA((6,)),
            pltpu.SemaphoreType.DMA((8,)),
            pltpu.SemaphoreType.DMA,
        ],
        compiler_params=pltpu.CompilerParams(collective_id=0, has_side_effects=True),
    )(own)


def attend_kernel(block_ref, q_ref, k_ref, v_ref, o_ref, qe, acc, top):
    scale = HEAD ** (-0.5) * 1.4426950408889634
    heads = q_ref.shape[1]
    rows = heads * ROWS
    sub = 256
    for part in range(2):
        block = block_ref[part]
        q = q_ref[part].reshape(rows, HEAD).astype(jnp.float32) * scale
        q_hi = q.astype(jnp.bfloat16)
        qe[:, :HEAD] = q_hi
        qe[:, HEAD:] = (q - q_hi.astype(jnp.float32)).astype(jnp.bfloat16)
        acc[...] = jnp.zeros_like(acc)
        top[...] = jnp.full_like(top, -1e30)

        def step(j, masked):
            first = pl.multiple_of(j * CHUNK, CHUNK)
            k = k_ref[pl.ds(first, CHUNK), :]
            v = v_ref[pl.ds(first, CHUNK), :]
            ke = jnp.concatenate([k, k], axis=1)
            ve = jnp.concatenate([v, jnp.ones_like(v)], axis=1)
            for r in range(rows // sub):
                here = pl.ds(r * sub, sub)
                s = lax.dot_general(
                    qe[here, :], ke, (((1,), (1,)), ((), ())), preferred_element_type=jnp.float32
                )
                if masked:
                    row = lax.broadcasted_iota(jnp.int32, s.shape, 0) % ROWS + block * ROWS
                    col = lax.broadcasted_iota(jnp.int32, s.shape, 1) + first
                    s = jnp.where(col <= row, s, -1e30)
                old = top[here, :]
                new = jnp.maximum(old, jnp.max(s, axis=1, keepdims=True))
                top[here, :] = new
                weights = jnp.exp2(s - new[:, :1]).astype(jnp.bfloat16)
                fade = jnp.exp2(old - new)
                o = jnp.dot(weights, ve, preferred_element_type=jnp.float32)
                acc[here, :] = acc[here, :] * jnp.concatenate([fade, fade], axis=1) + o

        whole = block * ROWS // CHUNK

        def body(j, _):
            step(j, False)
            return 0

        lax.fori_loop(0, whole, body, 0)
        step(whole, True)
        for h in range(heads):
            here = pl.ds(h * ROWS, ROWS)
            o_ref[part * ROWS : (part + 1) * ROWS, h * HEAD : (h + 1) * HEAD] = (
                acc[here, :HEAD] / acc[here, HEAD:]
            ).astype(jnp.bfloat16)


def attend(blocks, q, k, v):
    heads = q.shape[1]
    rows = heads * ROWS
    vmem = pl.BlockSpec(memory_space=pltpu.VMEM)
    return pl.pallas_call(
        attend_kernel,
        out_shape=jax.ShapeDtypeStruct((2 * ROWS, heads * HEAD), jnp.bfloat16),
        in_specs=[pl.BlockSpec(memory_space=pltpu.SMEM), vmem, vmem, vmem],
        out_specs=vmem,
        scratch_shapes=[
            pltpu.VMEM((rows, 2 * HEAD), jnp.bfloat16),
            pltpu.VMEM((rows, 2 * HEAD), jnp.float32),
            pltpu.VMEM((rows, HEAD), jnp.float32),
        ],
        compiler_params=pltpu.CompilerParams(vmem_limit_bytes=40 << 20),
        cost_estimate=pl.CostEstimate(
            flops=2 * 2 * 17 * CHUNK * rows * 256, bytes_accessed=10 << 20, transcendentals=17 << 20
        ),
    )(blocks, q, k, v)


GROUP = 16
STEP = 32


def sort_matrix(turned):
    r = lax.broadcasted_iota(jnp.int32, (256, 256), 1 if turned else 0)
    j = lax.broadcasted_iota(jnp.int32, (256, 256), 0 if turned else 1)
    same = (r // 64 == j // 4 % 4) & (r // 4 % 16 == j // 16) & (r % 4 == j % 4)
    return jnp.where(same, 1.0, 0.0).astype(jnp.bfloat16)


def expert_kernel(a_ref, wg_ref, wu_ref, wd_ref, o_ref, x_ref, y_ref):
    gather, spread = sort_matrix(False), sort_matrix(True)
    for h in range(STEP // GROUP):
        for k in range(3):
            part = a_ref[h * GROUP : (h + 1) * GROUP, 16 * k : 16 * k + 16, :].reshape(256, 512)
            part = jnp.dot(gather, part, preferred_element_type=jnp.float32).astype(jnp.bfloat16)
            first = (h * 3 + k) * 64
            for q in range(4):
                x_ref[first : first + 64, q * 512 : (q + 1) * 512] = part[q * 64 : (q + 1) * 64]
    x = x_ref[...]
    gate = jnp.dot(x, wg_ref[...], preferred_element_type=jnp.float32)
    up = jnp.dot(x, wu_ref[...], preferred_element_type=jnp.float32)
    hidden = (gate / (1.0 + jnp.exp(-gate)) * up).astype(jnp.bfloat16)
    y_ref[...] = jnp.dot(hidden, wd_ref[...], preferred_element_type=jnp.float32).astype(
        jnp.bfloat16
    )
    for h in range(STEP // GROUP):
        for k in range(3):
            first = (h * 3 + k) * 64
            part = jnp.concatenate(
                [y_ref[first : first + 64, q * 512 : (q + 1) * 512] for q in range(4)], axis=0
            )
            part = jnp.dot(spread, part, preferred_element_type=jnp.float32).astype(jnp.bfloat16)
            o_ref[h * GROUP : (h + 1) * GROUP, 16 * k : 16 * k + 16, :] = part.reshape(
                GROUP, 16, 512
            )


def experts(arrived, wg, wu, wd):
    rows = STEP * CAP
    once = pl.Buffered(1)
    return pl.pallas_call(
        expert_kernel,
        grid=(DEVS // STEP,),
        out_shape=jax.ShapeDtypeStruct(arrived.shape, jnp.bfloat16),
        in_specs=[
            pl.BlockSpec((STEP, 48, 512), lambda i: (i, 0, 0)),
            pl.BlockSpec((WIDTH, FF), lambda i: (0, 0), pipeline_mode=once),
            pl.BlockSpec((WIDTH, FF), lambda i: (0, 0), pipeline_mode=once),
            pl.BlockSpec((FF, WIDTH), lambda i: (0, 0), pipeline_mode=once),
        ],
        out_specs=pl.BlockSpec((STEP, 48, 512), lambda i: (i, 0, 0)),
        scratch_shapes=[
            pltpu.VMEM((rows, WIDTH), jnp.bfloat16),
            pltpu.VMEM((rows, WIDTH), jnp.bfloat16),
        ],
        compiler_params=pltpu.CompilerParams(vmem_limit_bytes=40 << 20),
        cost_estimate=pl.CostEstimate(
            flops=6 * DEVS * CAP * WIDTH * FF, bytes_accessed=22 << 20, transcendentals=0
        ),
    )(arrived, wg, wu, wd)


def shards(
    tokens,
    ln1_gain,
    w_query,
    key_weight,
    value_weight,
    q_gain,
    k_gain,
    w_out,
    ln2_gain,
    expert_ids,
    route_weights,
    w_gate,
    w_up,
    w_down,
):
    f32, bf16 = jnp.float32, jnp.bfloat16
    me = lax.axis_index("ctx") * 8 + lax.axis_index("exp")
    core = lax.axis_index("ctx") % 2
    partner = [(i, DEVS - 1 - i) for i in range(DEVS)]

    def across(turn):
        return [(i, i ^ turn) for i in range(8)]

    siblings = [(i, i ^ 1) for i in range(16)]

    q_half = lax.dynamic_slice_in_dim(w_query, core * HEAD, HEAD, 1)
    q_got = [lax.ppermute(q_half, "exp", across(t)) for t in (1, 2, 3)]
    q_other = [lax.ppermute(w, "ctx", siblings) for w in q_got]

    inputs32 = tokens.astype(f32)
    normed = rms_scale(inputs32, ln1_gain).astype(bf16)
    normed_partner = lax.ppermute(normed, BOTH, partner)
    cos, sin = rope_tables(me * ROWS)
    cos_p, sin_p = rope_tables((DEVS - 1 - me) * ROWS)

    kv = jnp.dot(
        normed, jnp.concatenate([key_weight, value_weight], axis=1), preferred_element_type=f32
    )
    both = []
    for g in range(KV_HEADS):
        k = rotate(rms_scale(kv[:, g * HEAD : (g + 1) * HEAD], k_gain), cos, sin).astype(bf16)
        v = kv[:, (KV_HEADS + g) * HEAD : (KV_HEADS + g + 1) * HEAD].astype(bf16)
        both.append(jnp.stack([k, v]))
    gathered = gather_kv(jnp.stack(both)).reshape(2, DEVS * ROWS, HEAD)

    weights = jnp.concatenate([w_query] + q_got + q_other, axis=1)
    heads = weights.shape[1] // HEAD

    def queries_of(rows, cos, sin):
        q = jnp.dot(rows, weights, preferred_element_type=f32)
        q = q.reshape(ROWS, heads, HEAD).transpose(1, 0, 2)
        return rotate(rms_scale(q, q_gain), cos, sin).astype(bf16)

    queries = jnp.stack([queries_of(normed, cos, sin), queries_of(normed_partner, cos_p, sin_p)])
    blocks = jnp.stack([me, DEVS - 1 - me]).astype(jnp.int32)
    attended = attend(blocks, queries, gathered[0], gathered[1])

    o_half = lax.dynamic_slice_in_dim(w_out, core * HEAD, HEAD, 0)
    o_got = [lax.ppermute(o_half, "exp", across(t)) for t in (1, 2, 3)]
    o_other = [lax.ppermute(w, "ctx", siblings) for w in o_got]
    out_weights = jnp.concatenate([w_out] + o_got + o_other, axis=0)
    theirs = jnp.dot(attended[ROWS:], out_weights, preferred_element_type=f32).astype(bf16)
    theirs = lax.ppermute(theirs, BOTH, partner)
    mine = jnp.dot(attended[:ROWS], out_weights, preferred_element_type=f32)
    residual = (inputs32 + (mine + theirs.astype(f32))).astype(bf16)
    normed2 = rms_scale(residual.astype(f32), ln2_gain).astype(bf16)

    chosen = expert_ids[:, :, None] == jnp.arange(DEVS)[None, None, :]
    counts = jnp.any(chosen, axis=1)
    before = jnp.arange(ROWS)[:, None] > jnp.arange(ROWS)[None, :]
    rank = jnp.dot(before.astype(bf16), counts.astype(bf16), preferred_element_type=f32)
    slots = jnp.where(counts, rank, -1.0).T
    route = jnp.sum(
        jnp.where(chosen, (route_weights.astype(f32) / 1024.0)[:, :, None], 0.0), axis=1
    ).T
    row = jnp.arange(48)
    row_slot = (row // 16 * 4 + row % 4).astype(f32)
    row_part = row // 4 % 4
    hot = (jnp.tile(slots, (1, 4))[:, None, :] == row_slot[None, :, None]) & (
        row_part[None, :, None] == (jnp.arange(512) // ROWS)[None, None, :]
    )
    dispatch = hot.astype(bf16).reshape(DEVS * 48, 512)
    combine = (
        jnp.where(hot, jnp.tile(route, (1, 4))[:, None, :], 0.0)
        .astype(bf16)
        .reshape(DEVS * 48, 512)
    )
    parts = normed2.reshape(ROWS, 4, 512).transpose(1, 0, 2).reshape(512, 512)
    outgoing = jnp.dot(dispatch, parts, preferred_element_type=f32).astype(bf16)
    arrived = lax.all_to_all(outgoing, BOTH, split_axis=0, concat_axis=0, tiled=True)
    produced = experts(arrived.reshape(DEVS, 48, 512), w_gate[0], w_up[0], w_down[0])
    returned = lax.all_to_all(
        produced.reshape(DEVS * 48, 512), BOTH, split_axis=0, concat_axis=0, tiled=True
    )
    mixture = lax.dot_general(
        combine, returned, (((0,), (0,)), ((), ())), preferred_element_type=f32
    )
    mixture = mixture.reshape(4, ROWS, 512).transpose(1, 0, 2).reshape(ROWS, WIDTH)
    return (residual.astype(f32) + mixture).astype(bf16)


def solution(mesh):
    two = P(BOTH, None)
    three = P(BOTH, None, None)
    in_specs = (
        two,
        P(),
        P(None, "exp"),
        P(),
        P(),
        P(),
        P(),
        P("exp", None),
        P(),
        two,
        two,
        three,
        three,
        three,
    )
    return jax.shard_map(shards, mesh=mesh, in_specs=in_specs, out_specs=two, check_vma=False)
```

```python
import jax
import jax.numpy as jnp
from jax import lax
from jax.experimental import pallas as pl
from jax.experimental.pallas import tpu as pltpu
from jax.sharding import PartitionSpec as P

HEAD = 128
KV_HEADS = 2
QUERY_HEADS = 16
TOP = 8
CAP = 12
ROWS = 128
WIDTH = 2048
FF = 768
DEVS = 128
EPS = 1e-06
THETA = 1000000.0
CHUNK = 1024
BOTH = ("ctx", "exp")
MESH = pl.DeviceIdType.MESH


def rope_tables(first):
    half = HEAD // 2
    frequency = THETA ** (-2.0 * jnp.arange(half, dtype=jnp.float32) / HEAD)
    positions = (first + jnp.arange(ROWS)).astype(jnp.float32)
    angles = positions[:, None] * frequency[None, :]
    return jnp.cos(angles), jnp.sin(angles)


def place():
    c, e = lax.axis_index("ctx"), lax.axis_index("exp")
    return e // 2, (c // 2) % 2 * 2 + e % 2, c // 4, c % 2


def ids(x, y, z, core):
    return ((z * 2 + y // 2) * 2 + core, x * 2 + y % 2)


def norm_rows(v, gain):
    return v * lax.rsqrt(jnp.mean(v * v, axis=-1, keepdims=True) + EPS) * gain


def turn(v, cos, sin):
    return v * cos + pltpu.roll(v, HEAD // 2, 1) * sin


def layer_kernel(
    tokens,
    ln1,
    w_query,
    w_key,
    w_value,
    q_gain,
    k_gain,
    w_out,
    ln2,
    cos,
    sin,
    residual,
    normed2,
    normed,
    own,
    buf,
    wq,
    wo,
    qe,
    acc,
    top,
    attended,
    leaving,
    landing,
    kept,
    out_sem,
    in_sem,
):
    f32, bf16 = jnp.float32, jnp.bfloat16
    x, y, z, c = place()
    yh, yl = y // 2, y % 2
    b = lax.axis_index("ctx") * 8 + lax.axis_index("exp")
    x1, y1 = x + 1 - 2 * (x % 2), y + 1 - 2 * (y % 2)
    near = [(lax.rem(x + dx, 4), lax.rem(c + dc, 2)) for dc in range(2) for dx in range(4)]
    ys = [lax.rem(y + d, 4) for d in range(1, 4)]
    zs = [lax.rem(z + d, 4) for d in range(1, 4)]
    other = ids(x, y, z, 1 - c)
    partner = ids(3 - x, 3 - y, 3 - z, 1 - c)
    beside, along, diagonal = ids(x, y1, z, c), ids(x1, y, z, c), ids(x1, y1, z, c)

    barrier = pltpu.get_barrier_semaphore()
    peers = [ids(px, y, z, pc) for px, pc in near[1:]]
    peers += [ids(x, py, z, c) for py in ys] + [ids(x, y, pz, c) for pz in zs]
    peers += [partner, diagonal]
    for peer in peers:
        pl.semaphore_signal(barrier, inc=1, device_id=peer, device_id_type=MESH)

    sent = []

    def send(src, dst, peer):
        copy = pltpu.make_async_remote_copy(
            src_ref=src,
            dst_ref=dst,
            send_sem=out_sem.at[len(sent)],
            recv_sem=in_sem.at[len(sent)],
            device_id=peer,
            device_id_type=MESH,
        )
        copy.start()
        sent.append(copy)
        return copy

    rows = norm_rows(tokens[...].astype(f32), ln1[...]).astype(bf16)
    normed[0] = rows
    keys = jnp.dot(rows, w_key[...], preferred_element_type=f32)
    values = jnp.dot(rows, w_value[...], preferred_element_type=f32).astype(bf16)
    for g in range(KV_HEADS):
        k = norm_rows(keys[:, g * HEAD : (g + 1) * HEAD], k_gain[...])
        own[g, 0] = turn(k, cos[0], sin[0]).astype(bf16)
        own[g, 1] = values[:, g * HEAD : (g + 1) * HEAD]
    buf[c, z, yh, c, x, yl] = own[x // 2, c]
    pl.semaphore_wait(barrier, len(peers))

    first = []
    for px, pc in near[1:]:
        first.append(
            send(own.at[px // 2, pc], buf.at[pc, z, yh, c, x, yl], ids(px, y, z, pc))
        )
    half = w_query.at[:, pl.ds(pl.multiple_of(c * HEAD, HEAD), HEAD)]
    q1 = send(half, wq.at[0, c], beside)
    q2 = send(half, wq.at[1, c], along)
    swap = send(normed.at[0], normed.at[1], partner)
    for copy in first:
        copy.wait_recv()

    low, high = pl.ds(0, 2), pl.ds(2, 2)
    two, four = pl.ds(0, 2), pl.ds(0, 4)
    a1 = buf.at[c, z, yh, two, low, yl]
    b1 = buf.at[c, z, yh, two, high, yl]
    second = [send(a1, a1, ids(x, py, z, c)) for py in ys]
    second += [send(b1, b1, ids(x, y, pz, c)) for pz in zs]
    for copy in second:
        copy.wait_recv()

    def of_z(pz, part=two):
        return buf.at[c, pz, part, two, low, two]

    def of_y(py, part=four):
        return buf.at[c, part, py // 2, two, high, py % 2]

    up_z, down_z, up_y, down_y = zs[0], zs[2], ys[0], ys[2]
    third = [
        send(of_z(z), of_z(z), ids(x, y, up_z, c)),
        send(of_z(z), of_z(z), ids(x, y, down_z, c)),
        send(of_y(y), of_y(y), ids(x, up_y, z, c)),
        send(of_y(y), of_y(y), ids(x, down_y, z, c)),
    ]
    handed = [send(of_z(z), of_z(z), other), send(of_y(y), of_y(y), other)]
    q1.wait_recv()
    q3 = send(wq.at[0, c], wq.at[2, c], along)
    handed_q = [send(wq.at[0, c], wq.at[0, c], other)]
    q2.wait_recv()
    handed_q.append(send(wq.at[1, c], wq.at[1, c], other))

    third[0].wait_recv()
    part = of_z(down_z, pl.ds(0, 1))
    fourth = [send(part, part, ids(x, y, up_z, c))]
    handed.append(send(of_z(down_z), of_z(down_z), other))
    third[1].wait_recv()
    part = of_z(up_z, pl.ds(1, 1))
    fourth.append(send(part, part, ids(x, y, down_z, c)))
    handed.append(send(of_z(up_z), of_z(up_z), other))
    third[2].wait_recv()
    part = of_y(down_y, pl.ds(0, 2))
    fourth.append(send(part, part, ids(x, up_y, z, c)))
    handed.append(send(of_y(down_y), of_y(down_y), other))
    third[3].wait_recv()
    part = of_y(up_y, pl.ds(2, 2))
    fourth.append(send(part, part, ids(x, down_y, z, c)))
    handed.append(send(of_y(up_y), of_y(up_y), other))

    scale = HEAD ** (-0.5) * 1.4426950408889634

    def queries(index, weights):
        both = jnp.dot(
            normed[...].reshape(2 * ROWS, WIDTH), weights, preferred_element_type=f32
        )
        for h in range(2):
            for p in range(2):
                v = both[p * ROWS : (p + 1) * ROWS, h * HEAD : (h + 1) * HEAD]
                v = turn(norm_rows(v, q_gain[...]), cos[p], sin[p]).astype(bf16)
                v = v.astype(f32) * scale
                v_hi = v.astype(bf16)
                here = pl.ds((index * 2 + h) * ROWS, ROWS)
                qe[p, here, :HEAD] = v_hi
                qe[p, here, HEAD:] = (v - v_hi.astype(f32)).astype(bf16)

    swap.wait_recv()
    queries(0, w_query[...])
    q3.wait_recv()
    handed_q.append(send(wq.at[2, c], wq.at[2, c], other))
    for t in range(2):
        handed_q[t].wait_recv()
        queries(t + 1, jnp.concatenate([wq[t, 0], wq[t, 1]], axis=1))
    fourth[0].wait_recv()
    far = lax.rem(z + 2, 4)
    handed.append(send(of_z(far, pl.ds(0, 1)), of_z(far, pl.ds(0, 1)), other))
    fourth[1].wait_recv()
    handed.append(send(of_z(far, pl.ds(1, 1)), of_z(far, pl.ds(1, 1)), other))
    fourth[2].wait_recv()
    far = lax.rem(y + 2, 4)
    handed.append(send(of_y(far, pl.ds(0, 2)), of_y(far, pl.ds(0, 2)), other))
    fourth[3].wait_recv()
    handed.append(send(of_y(far, pl.ds(2, 2)), of_y(far, pl.ds(2, 2)), other))
    out_half = w_out.at[pl.ds(pl.multiple_of(c * HEAD, HEAD), HEAD), :]
    out_got = [
        send(out_half, wo.at[t, c], peer) for t, peer in enumerate((beside, along, diagonal))
    ]
    handed_q[2].wait_recv()
    queries(3, jnp.concatenate([wq[2, 0], wq[2, 1]], axis=1))
    for copy in handed:
        copy.wait_recv()

    heads = QUERY_HEADS // KV_HEADS
    tall = heads * ROWS
    sub = 256
    for p in range(2):
        block = b if p == 0 else DEVS - 1 - b
        acc[...] = jnp.zeros_like(acc)
        top[...] = jnp.full_like(top, -1e30)

        def step(j, masked, p=p, block=block):
            k = buf[0, j // 4, j // 2 % 2, j % 2].reshape(CHUNK, HEAD)
            v = buf[1, j // 4, j // 2 % 2, j % 2].reshape(CHUNK, HEAD)
            ke = jnp.concatenate([k, k], axis=1)
            ve = jnp.concatenate([v, jnp.ones_like(v)], axis=1)
            for r in range(tall // sub):
                here = pl.ds(r * sub, sub)
                s = lax.dot_general(
                    qe[p, here, :], ke, (((1,), (1,)), ((), ())), preferred_element_type=f32
                )
                if masked:
                    row = lax.broadcasted_iota(jnp.int32, s.shape, 0) % ROWS + block * ROWS
                    col = lax.broadcasted_iota(jnp.int32, s.shape, 1) + j * CHUNK
                    s = jnp.where(col <= row, s, -1e30)
                old = top[here, :]
                new = jnp.maximum(old, jnp.max(s, axis=1, keepdims=True))
                top[here, :] = new
                weights = jnp.exp2(s - new[:, :1]).astype(bf16)
                fade = jnp.exp2(old - new)
                o = jnp.dot(weights, ve, preferred_element_type=f32)
                acc[here, :] = acc[here, :] * jnp.concatenate([fade, fade], axis=1) + o

        whole = block // (CHUNK // ROWS)

        def body(j, _, step=step):
            step(j, False)
            return 0

        lax.fori_loop(0, whole, body, 0)
        step(whole, True)
        for h in range(heads):
            here = pl.ds(h * ROWS, ROWS)
            attended[p * ROWS : (p + 1) * ROWS, h * HEAD : (h + 1) * HEAD] = (
                acc[here, :HEAD] / acc[here, HEAD:]
            ).astype(bf16)

    handed_o = []
    for t in range(3):
        out_got[t].wait_recv()
        handed_o.append(send(wo.at[t, c], wo.at[t, c], other))
    for copy in handed_o:
        copy.wait_recv()
    back = []
    wide = 512
    for n in range(WIDTH // wide):
        here = pl.ds(n * wide, wide)
        o = jnp.dot(attended[:, : 2 * HEAD], w_out[:, here], preferred_element_type=f32)
        for t in range(3):
            o = o + jnp.dot(
                attended[:, (t + 1) * 2 * HEAD : (t + 2) * 2 * HEAD],
                wo[t, :, :, here].reshape(2 * HEAD, wide),
                preferred_element_type=f32,
            )
        leaving[n] = o[ROWS:].astype(bf16)
        kept[:, here] = o[:ROWS]
        back.append(send(leaving.at[n], landing.at[n], partner))
    total = jnp.zeros((ROWS, 1), f32)
    for n in range(WIDTH // wide):
        here = pl.ds(n * wide, wide)
        back[n].wait_recv()
        r = tokens[:, here].astype(f32) + (kept[:, here] + landing[n].astype(f32))
        r = r.astype(bf16)
        residual[:, here] = r
        r = r.astype(f32)
        total = total + jnp.sum(r * r, axis=-1, keepdims=True)
    r = residual[...].astype(f32)
    normed2[...] = (r * lax.rsqrt(total * (1.0 / WIDTH) + EPS) * ln2[...]).astype(bf16)
    for copy in sent:
        copy.wait_send()


def before_experts(*args):
    f32, bf16 = jnp.float32, jnp.bfloat16
    vmem = pl.BlockSpec(memory_space=pltpu.VMEM)
    rows = QUERY_HEADS // KV_HEADS * ROWS
    made = jax.ShapeDtypeStruct((ROWS, WIDTH), bf16)
    copies = 64
    return pl.pallas_call(
        layer_kernel,
        out_shape=(made, made),
        in_specs=[vmem] * len(args),
        out_specs=(vmem, vmem),
        scratch_shapes=[
            pltpu.VMEM((2, ROWS, WIDTH), bf16),
            pltpu.VMEM((KV_HEADS, 2, ROWS, HEAD), bf16),
            pltpu.VMEM((2, 4, 2, 2, 4, 2, ROWS, HEAD), bf16),
            pltpu.VMEM((3, 2, WIDTH, HEAD), bf16),
            pltpu.VMEM((3, 2, HEAD, WIDTH), bf16),
            pltpu.VMEM((2, rows, 2 * HEAD), bf16),
            pltpu.VMEM((rows, 2 * HEAD), f32),
            pltpu.VMEM((rows, HEAD), f32),
            pltpu.VMEM((2 * ROWS, rows), bf16),
            pltpu.VMEM((4, ROWS, 512), bf16),
            pltpu.VMEM((4, ROWS, 512), bf16),
            pltpu.VMEM((ROWS, WIDTH), f32),
            pltpu.SemaphoreType.DMA((copies,)),
            pltpu.SemaphoreType.DMA((copies,)),
        ],
        compiler_params=pltpu.CompilerParams(
            collective_id=0, has_side_effects=True, vmem_limit_bytes=48 << 20
        ),
    )(*args)


GROUP = 16
STEP = 32


def sort_matrix(turned):
    r = lax.broadcasted_iota(jnp.int32, (256, 256), 1 if turned else 0)
    j = lax.broadcasted_iota(jnp.int32, (256, 256), 0 if turned else 1)
    same = (r // 64 == j // 4 % 4) & (r // 4 % 16 == j // 16) & (r % 4 == j % 4)
    return jnp.where(same, 1.0, 0.0).astype(jnp.bfloat16)


def expert_kernel(a_ref, wg_ref, wu_ref, wd_ref, o_ref, x_ref, y_ref):
    gather, spread = sort_matrix(False), sort_matrix(True)
    for h in range(STEP // GROUP):
        for k in range(3):
            part = a_ref[h * GROUP : (h + 1) * GROUP, 16 * k : 16 * k + 16, :].reshape(256, 512)
            part = jnp.dot(gather, part, preferred_element_type=jnp.float32).astype(jnp.bfloat16)
            first = (h * 3 + k) * 64
            for q in range(4):
                x_ref[first : first + 64, q * 512 : (q + 1) * 512] = part[q * 64 : (q + 1) * 64]
    x = x_ref[...]
    gate = jnp.dot(x, wg_ref[...], preferred_element_type=jnp.float32)
    up = jnp.dot(x, wu_ref[...], preferred_element_type=jnp.float32)
    hidden = (gate / (1.0 + jnp.exp(-gate)) * up).astype(jnp.bfloat16)
    y_ref[...] = jnp.dot(hidden, wd_ref[...], preferred_element_type=jnp.float32).astype(
        jnp.bfloat16
    )
    for h in range(STEP // GROUP):
        for k in range(3):
            first = (h * 3 + k) * 64
            part = jnp.concatenate(
                [y_ref[first : first + 64, q * 512 : (q + 1) * 512] for q in range(4)], axis=0
            )
            part = jnp.dot(spread, part, preferred_element_type=jnp.float32).astype(jnp.bfloat16)
            o_ref[h * GROUP : (h + 1) * GROUP, 16 * k : 16 * k + 16, :] = part.reshape(
                GROUP, 16, 512
            )


def experts(arrived, wg, wu, wd):
    rows = STEP * CAP
    once = pl.Buffered(1)
    return pl.pallas_call(
        expert_kernel,
        grid=(DEVS // STEP,),
        out_shape=jax.ShapeDtypeStruct(arrived.shape, jnp.bfloat16),
        in_specs=[
            pl.BlockSpec((STEP, 48, 512), lambda i: (i, 0, 0)),
            pl.BlockSpec((WIDTH, FF), lambda i: (0, 0), pipeline_mode=once),
            pl.BlockSpec((WIDTH, FF), lambda i: (0, 0), pipeline_mode=once),
            pl.BlockSpec((FF, WIDTH), lambda i: (0, 0), pipeline_mode=once),
        ],
        out_specs=pl.BlockSpec((STEP, 48, 512), lambda i: (i, 0, 0)),
        scratch_shapes=[
            pltpu.VMEM((rows, WIDTH), jnp.bfloat16),
            pltpu.VMEM((rows, WIDTH), jnp.bfloat16),
        ],
        compiler_params=pltpu.CompilerParams(vmem_limit_bytes=40 << 20),
        cost_estimate=pl.CostEstimate(
            flops=6 * DEVS * CAP * WIDTH * FF, bytes_accessed=22 << 20, transcendentals=0
        ),
    )(arrived, wg, wu, wd)


def shards(
    tokens,
    ln1_gain,
    w_query,
    key_weight,
    value_weight,
    q_gain,
    k_gain,
    w_out,
    ln2_gain,
    expert_ids,
    route_weights,
    w_gate,
    w_up,
    w_down,
):
    f32, bf16 = jnp.float32, jnp.bfloat16
    me = lax.axis_index("ctx") * 8 + lax.axis_index("exp")
    tables = [rope_tables(first * ROWS) for first in (me, DEVS - 1 - me)]
    cos = jnp.stack([jnp.concatenate([c, c], axis=1) for c, s in tables])
    sin = jnp.stack([jnp.concatenate([-s, s], axis=1) for c, s in tables])
    residual, normed2 = before_experts(
        tokens,
        ln1_gain.reshape(1, WIDTH),
        w_query,
        key_weight,
        value_weight,
        q_gain.reshape(1, HEAD),
        k_gain.reshape(1, HEAD),
        w_out,
        ln2_gain.reshape(1, WIDTH),
        cos,
        sin,
    )

    chosen = expert_ids[:, :, None] == jnp.arange(DEVS)[None, None, :]
    counts = jnp.any(chosen, axis=1)
    before = jnp.arange(ROWS)[:, None] > jnp.arange(ROWS)[None, :]
    rank = jnp.dot(before.astype(bf16), counts.astype(bf16), preferred_element_type=f32)
    slots = jnp.where(counts, rank, -1.0).T
    route = jnp.sum(
        jnp.where(chosen, (route_weights.astype(f32) / 1024.0)[:, :, None], 0.0), axis=1
    ).T
    row = jnp.arange(48)
    row_slot = (row // 16 * 4 + row % 4).astype(f32)
    row_part = row // 4 % 4
    hot = (jnp.tile(slots, (1, 4))[:, None, :] == row_slot[None, :, None]) & (
        row_part[None, :, None] == (jnp.arange(512) // ROWS)[None, None, :]
    )
    dispatch = hot.astype(bf16).reshape(DEVS * 48, 512)
    combine = (
        jnp.where(hot, jnp.tile(route, (1, 4))[:, None, :], 0.0)
        .astype(bf16)
        .reshape(DEVS * 48, 512)
    )
    parts = normed2.reshape(ROWS, 4, 512).transpose(1, 0, 2).reshape(512, 512)
    outgoing = jnp.dot(dispatch, parts, preferred_element_type=f32).astype(bf16)
    arrived = lax.all_to_all(outgoing, BOTH, split_axis=0, concat_axis=0, tiled=True)
    produced = experts(arrived.reshape(DEVS, 48, 512), w_gate[0], w_up[0], w_down[0])
    returned = lax.all_to_all(
        produced.reshape(DEVS * 48, 512), BOTH, split_axis=0, concat_axis=0, tiled=True
    )
    mixture = lax.dot_general(
        combine, returned, (((0,), (0,)), ((), ())), preferred_element_type=f32
    )
    mixture = mixture.reshape(4, ROWS, 512).transpose(1, 0, 2).reshape(ROWS, WIDTH)
    return (residual.astype(f32) + mixture).astype(bf16)


def solution(mesh):
    two = P(BOTH, None)
    three = P(BOTH, None, None)
    in_specs = (
        two,
        P(),
        P(None, "exp"),
        P(),
        P(),
        P(),
        P(),
        P("exp", None),
        P(),
        two,
        two,
        three,
        three,
        three,
    )
    return jax.shard_map(shards, mesh=mesh, in_specs=in_specs, out_specs=two, check_vma=False)
```

```python
import jax
import jax.numpy as jnp
from jax import lax
from jax.experimental import pallas as pl
from jax.experimental.pallas import tpu as pltpu
from jax.sharding import PartitionSpec as P

HEAD = 128
KV_HEADS = 2
QUERY_HEADS = 16
ROWS = 128
WIDTH = 2048
FF = 768
DEVS = 128
EPS = 1e-06
THETA = 1000000.0
CHUNK = 1024
BOTH = ("ctx", "exp")
MESH = pl.DeviceIdType.MESH


def rope_tables(first):
    half = HEAD // 2
    frequency = THETA ** (-2.0 * jnp.arange(half, dtype=jnp.float32) / HEAD)
    positions = (first + jnp.arange(ROWS)).astype(jnp.float32)
    angles = positions[:, None] * frequency[None, :]
    return jnp.cos(angles), jnp.sin(angles)


def place():
    c, e = lax.axis_index("ctx"), lax.axis_index("exp")
    return e // 2, (c // 2) % 2 * 2 + e % 2, c // 4, c % 2


def ids(x, y, z, core):
    return ((z * 2 + y // 2) * 2 + core, x * 2 + y % 2)


def norm_rows(v, gain):
    return v * lax.rsqrt(jnp.mean(v * v, axis=-1, keepdims=True) + EPS) * gain


def turn(v, cos, sin):
    return v * cos + pltpu.roll(v, HEAD // 2, 1) * sin


def layer_kernel(
    tokens,
    ln1,
    w_query,
    w_key,
    w_value,
    q_gain,
    k_gain,
    w_out,
    ln2,
    cos,
    sin,
    residual,
    normed2,
    normed,
    own,
    buf,
    wq,
    wo,
    qe,
    acc,
    top,
    attended,
    leaving,
    landing,
    kept,
    out_sem,
    in_sem,
):
    f32, bf16 = jnp.float32, jnp.bfloat16
    x, y, z, c = place()
    yh, yl = y // 2, y % 2
    b = lax.axis_index("ctx") * 8 + lax.axis_index("exp")
    x1, y1 = x + 1 - 2 * (x % 2), y + 1 - 2 * (y % 2)
    near = [(lax.rem(x + dx, 4), lax.rem(c + dc, 2)) for dc in range(2) for dx in range(4)]
    ys = [lax.rem(y + d, 4) for d in range(1, 4)]
    zs = [lax.rem(z + d, 4) for d in range(1, 4)]
    other = ids(x, y, z, 1 - c)
    partner = ids(3 - x, 3 - y, 3 - z, 1 - c)
    beside, along, diagonal = ids(x, y1, z, c), ids(x1, y, z, c), ids(x1, y1, z, c)

    barrier = pltpu.get_barrier_semaphore()
    peers = [ids(px, y, z, pc) for px, pc in near[1:]]
    peers += [ids(x, py, z, c) for py in ys] + [ids(x, y, pz, c) for pz in zs]
    peers += [partner, diagonal]
    for peer in peers:
        pl.semaphore_signal(barrier, inc=1, device_id=peer, device_id_type=MESH)

    sent = []

    def send(src, dst, peer):
        copy = pltpu.make_async_remote_copy(
            src_ref=src,
            dst_ref=dst,
            send_sem=out_sem.at[len(sent)],
            recv_sem=in_sem.at[len(sent)],
            device_id=peer,
            device_id_type=MESH,
        )
        copy.start()
        sent.append(copy)
        return copy

    rows = norm_rows(tokens[...].astype(f32), ln1[...]).astype(bf16)
    normed[0] = rows
    keys = jnp.dot(rows, w_key[...], preferred_element_type=f32)
    values = jnp.dot(rows, w_value[...], preferred_element_type=f32).astype(bf16)
    for g in range(KV_HEADS):
        k = norm_rows(keys[:, g * HEAD : (g + 1) * HEAD], k_gain[...])
        own[g, 0] = turn(k, cos[0], sin[0]).astype(bf16)
        own[g, 1] = values[:, g * HEAD : (g + 1) * HEAD]
    buf[c, z, yh, c, x, yl] = own[x // 2, c]
    pl.semaphore_wait(barrier, len(peers))

    first = []
    for px, pc in near[1:]:
        first.append(
            send(own.at[px // 2, pc], buf.at[pc, z, yh, c, x, yl], ids(px, y, z, pc))
        )
    half = w_query.at[:, pl.ds(pl.multiple_of(c * HEAD, HEAD), HEAD)]
    q1 = send(half, wq.at[0, c], beside)
    q2 = send(half, wq.at[1, c], along)
    swap = send(normed.at[0], normed.at[1], partner)
    for copy in first:
        copy.wait_recv()

    low, high = pl.ds(0, 2), pl.ds(2, 2)
    two, four = pl.ds(0, 2), pl.ds(0, 4)
    a1 = buf.at[c, z, yh, two, low, yl]
    b1 = buf.at[c, z, yh, two, high, yl]
    second = [send(a1, a1, ids(x, py, z, c)) for py in ys]
    second += [send(b1, b1, ids(x, y, pz, c)) for pz in zs]
    for copy in second:
        copy.wait_recv()

    def of_z(pz, part=two):
        return buf.at[c, pz, part, two, low, two]

    def of_y(py, part=four):
        return buf.at[c, part, py // 2, two, high, py % 2]

    up_z, down_z, up_y, down_y = zs[0], zs[2], ys[0], ys[2]
    third = [
        send(of_z(z), of_z(z), ids(x, y, up_z, c)),
        send(of_z(z), of_z(z), ids(x, y, down_z, c)),
        send(of_y(y), of_y(y), ids(x, up_y, z, c)),
        send(of_y(y), of_y(y), ids(x, down_y, z, c)),
    ]
    handed = [send(of_z(z), of_z(z), other), send(of_y(y), of_y(y), other)]
    q1.wait_recv()
    q3 = send(wq.at[0, c], wq.at[2, c], along)
    handed_q = [send(wq.at[0, c], wq.at[0, c], other)]
    q2.wait_recv()
    handed_q.append(send(wq.at[1, c], wq.at[1, c], other))

    third[0].wait_recv()
    part = of_z(down_z, pl.ds(0, 1))
    fourth = [send(part, part, ids(x, y, up_z, c))]
    handed.append(send(of_z(down_z), of_z(down_z), other))
    third[1].wait_recv()
    part = of_z(up_z, pl.ds(1, 1))
    fourth.append(send(part, part, ids(x, y, down_z, c)))
    handed.append(send(of_z(up_z), of_z(up_z), other))
    third[2].wait_recv()
    part = of_y(down_y, pl.ds(0, 2))
    fourth.append(send(part, part, ids(x, up_y, z, c)))
    handed.append(send(of_y(down_y), of_y(down_y), other))
    third[3].wait_recv()
    part = of_y(up_y, pl.ds(2, 2))
    fourth.append(send(part, part, ids(x, down_y, z, c)))
    handed.append(send(of_y(up_y), of_y(up_y), other))

    scale = HEAD ** (-0.5) * 1.4426950408889634

    def queries(index, weights):
        both = jnp.dot(
            normed[...].reshape(2 * ROWS, WIDTH), weights, preferred_element_type=f32
        )
        for h in range(2):
            for p in range(2):
                v = both[p * ROWS : (p + 1) * ROWS, h * HEAD : (h + 1) * HEAD]
                v = turn(norm_rows(v, q_gain[...]), cos[p], sin[p]).astype(bf16)
                v = v.astype(f32) * scale
                v_hi = v.astype(bf16)
                here = pl.ds((index * 2 + h) * ROWS, ROWS)
                qe[p, here, :HEAD] = v_hi
                qe[p, here, HEAD:] = (v - v_hi.astype(f32)).astype(bf16)

    swap.wait_recv()
    queries(0, w_query[...])
    q3.wait_recv()
    handed_q.append(send(wq.at[2, c], wq.at[2, c], other))
    for t in range(2):
        handed_q[t].wait_recv()
        queries(t + 1, jnp.concatenate([wq[t, 0], wq[t, 1]], axis=1))
    fourth[0].wait_recv()
    far = lax.rem(z + 2, 4)
    handed.append(send(of_z(far, pl.ds(0, 1)), of_z(far, pl.ds(0, 1)), other))
    fourth[1].wait_recv()
    handed.append(send(of_z(far, pl.ds(1, 1)), of_z(far, pl.ds(1, 1)), other))
    fourth[2].wait_recv()
    far = lax.rem(y + 2, 4)
    handed.append(send(of_y(far, pl.ds(0, 2)), of_y(far, pl.ds(0, 2)), other))
    fourth[3].wait_recv()
    handed.append(send(of_y(far, pl.ds(2, 2)), of_y(far, pl.ds(2, 2)), other))
    out_half = w_out.at[pl.ds(pl.multiple_of(c * HEAD, HEAD), HEAD), :]
    out_got = [
        send(out_half, wo.at[t, c], peer) for t, peer in enumerate((beside, along, diagonal))
    ]
    handed_q[2].wait_recv()
    queries(3, jnp.concatenate([wq[2, 0], wq[2, 1]], axis=1))
    for copy in handed:
        copy.wait_recv()

    heads = QUERY_HEADS // KV_HEADS
    tall = heads * ROWS
    sub = 256
    for p in range(2):
        block = b if p == 0 else DEVS - 1 - b
        acc[...] = jnp.zeros_like(acc)
        top[...] = jnp.full_like(top, -1e30)

        def step(j, masked, p=p, block=block):
            k = buf[0, j // 4, j // 2 % 2, j % 2].reshape(CHUNK, HEAD)
            v = buf[1, j // 4, j // 2 % 2, j % 2].reshape(CHUNK, HEAD)
            ke = jnp.concatenate([k, k], axis=1)
            ve = jnp.concatenate([v, jnp.ones_like(v)], axis=1)
            for r in range(tall // sub):
                here = pl.ds(r * sub, sub)
                s = lax.dot_general(
                    qe[p, here, :], ke, (((1,), (1,)), ((), ())), preferred_element_type=f32
                )
                if masked:
                    row = lax.broadcasted_iota(jnp.int32, s.shape, 0) % ROWS + block * ROWS
                    col = lax.broadcasted_iota(jnp.int32, s.shape, 1) + j * CHUNK
                    s = jnp.where(col <= row, s, -1e30)
                old = top[here, :]
                new = jnp.maximum(old, jnp.max(s, axis=1, keepdims=True))
                top[here, :] = new
                weights = jnp.exp2(s - new[:, :1]).astype(bf16)
                fade = jnp.exp2(old - new)
                o = jnp.dot(weights, ve, preferred_element_type=f32)
                acc[here, :] = acc[here, :] * jnp.concatenate([fade, fade], axis=1) + o

        whole = block // (CHUNK // ROWS)

        def body(j, _, step=step):
            step(j, False)
            return 0

        lax.fori_loop(0, whole, body, 0)
        step(whole, True)
        for h in range(heads):
            here = pl.ds(h * ROWS, ROWS)
            attended[p * ROWS : (p + 1) * ROWS, h * HEAD : (h + 1) * HEAD] = (
                acc[here, :HEAD] / acc[here, HEAD:]
            ).astype(bf16)

    handed_o = []
    for t in range(3):
        out_got[t].wait_recv()
        handed_o.append(send(wo.at[t, c], wo.at[t, c], other))
    for copy in handed_o:
        copy.wait_recv()
    back = []
    wide = 512
    for n in range(WIDTH // wide):
        here = pl.ds(n * wide, wide)
        o = jnp.dot(attended[:, : 2 * HEAD], w_out[:, here], preferred_element_type=f32)
        for t in range(3):
            o = o + jnp.dot(
                attended[:, (t + 1) * 2 * HEAD : (t + 2) * 2 * HEAD],
                wo[t, :, :, here].reshape(2 * HEAD, wide),
                preferred_element_type=f32,
            )
        leaving[n] = o[ROWS:].astype(bf16)
        kept[:, here] = o[:ROWS]
        back.append(send(leaving.at[n], landing.at[n], partner))
    total = jnp.zeros((ROWS, 1), f32)
    for n in range(WIDTH // wide):
        here = pl.ds(n * wide, wide)
        back[n].wait_recv()
        r = tokens[:, here].astype(f32) + (kept[:, here] + landing[n].astype(f32))
        r = r.astype(bf16)
        residual[:, here] = r
        r = r.astype(f32)
        total = total + jnp.sum(r * r, axis=-1, keepdims=True)
    r = residual[...].astype(f32)
    normed2[...] = (r * lax.rsqrt(total * (1.0 / WIDTH) + EPS) * ln2[...]).astype(bf16)
    for copy in sent:
        copy.wait_send()


def before_experts(*args):
    f32, bf16 = jnp.float32, jnp.bfloat16
    vmem = pl.BlockSpec(memory_space=pltpu.VMEM)
    rows = QUERY_HEADS // KV_HEADS * ROWS
    made = jax.ShapeDtypeStruct((ROWS, WIDTH), bf16)
    copies = 64
    return pl.pallas_call(
        layer_kernel,
        out_shape=(made, made),
        in_specs=[vmem] * len(args),
        out_specs=(vmem, vmem),
        scratch_shapes=[
            pltpu.VMEM((2, ROWS, WIDTH), bf16),
            pltpu.VMEM((KV_HEADS, 2, ROWS, HEAD), bf16),
            pltpu.VMEM((2, 4, 2, 2, 4, 2, ROWS, HEAD), bf16),
            pltpu.VMEM((3, 2, WIDTH, HEAD), bf16),
            pltpu.VMEM((3, 2, HEAD, WIDTH), bf16),
            pltpu.VMEM((2, rows, 2 * HEAD), bf16),
            pltpu.VMEM((rows, 2 * HEAD), f32),
            pltpu.VMEM((rows, HEAD), f32),
            pltpu.VMEM((2 * ROWS, rows), bf16),
            pltpu.VMEM((4, ROWS, 512), bf16),
            pltpu.VMEM((4, ROWS, 512), bf16),
            pltpu.VMEM((ROWS, WIDTH), f32),
            pltpu.SemaphoreType.DMA((copies,)),
            pltpu.SemaphoreType.DMA((copies,)),
        ],
        compiler_params=pltpu.CompilerParams(
            collective_id=0, has_side_effects=True, vmem_limit_bytes=48 << 20
        ),
    )(*args)


CUTS = ((0, 768), (768, 640), (1408, 640))
ROUNDS = 3
PLANE = 32
ROUND_ROWS = 512


def line_at(p, d, x, y, z, c):
    if p == 0:
        return x, y, (z + d) % 4, c
    if p == 1:
        return x, (y + d) % 4, z, c
    return (x + d) % 4, y, z, c


def plane_at(p, i, x, y, z, c):
    a, b, dc = i % 4, i // 4 % 4, i // 16
    if p == 0:
        return (x + a) % 4, (y + b) % 4, z, (c + dc) % 2
    if p == 1:
        return (x + b) % 4, y, (z + a) % 4, (c + dc) % 2
    return x, (y + a) % 4, (z + b) % 4, (c + dc) % 2


def opposite(i):
    return (4 - i % 4) % 4 + (4 - i // 4 % 4) % 4 * 4 + i // 16 * 16


def reorder(p, turned):
    shape = (ROUND_ROWS, ROUND_ROWS)
    r = lax.broadcasted_iota(jnp.int32, shape, 1 if turned else 0)
    j = lax.broadcasted_iota(jnp.int32, shape, 0 if turned else 1)
    dz, dx, dy = r // 4 % 4, r // 16 % 4, r // 64 % 4
    inner, low, high = (dy, dz, dx) if p == 1 else (dx, dy, dz)
    same = j == r // 256 * 256 + high * 64 + low * 16 + inner * 4 + r % 4
    return jnp.where(same, 1.0, 0.0).astype(jnp.bfloat16)


def expert_kernel(
    table,
    rows,
    residual,
    w_gate,
    w_up,
    w_down,
    out,
    tables,
    held0,
    held1,
    held2,
    went0,
    went1,
    went2,
    came0,
    came1,
    came2,
    back0,
    back1,
    back2,
    sums0,
    sums1,
    sums2,
    gave0,
    gave1,
    gave2,
    got0,
    got1,
    got2,
    x_rows,
    y_rows,
    wg,
    wu,
    wd,
    w_sem,
    line_out,
    line_in,
    plane_out,
    plane_in,
):
    f32, bf16 = jnp.float32, jnp.bfloat16
    me = place()
    held, went, came = (held0, held1, held2), (went0, went1, went2), (came0, came1, came2)
    back, sums = (back0, back1, back2), (sums0, sums1, sums2)
    gave, got = (gave0, gave1, gave2), (got0, got1, got2)

    barrier = pltpu.get_barrier_semaphore()

    def greet(i, _):
        for p in range(3):
            pl.semaphore_signal(
                barrier, inc=1, device_id=ids(*plane_at(p, i, *me)), device_id_type=MESH
            )
        return 0

    lax.fori_loop(1, PLANE, greet, 0)
    loads = [
        pltpu.make_async_copy(src, dst, w_sem.at[n])
        for n, (src, dst) in enumerate(((w_gate, wg), (w_up, wu), (w_down, wd)))
    ]
    for load in loads:
        load.start()
    for p, (first, wide) in enumerate(CUTS):
        held[p][0] = rows[:, first : first + wide]
        tables[p, 0] = table[p, 0]
    pl.semaphore_wait(barrier, 3 * (PLANE - 1))

    def remote(src, dst, out_sem, in_sem, peer):
        return pltpu.make_async_remote_copy(
            src_ref=src,
            dst_ref=dst,
            send_sem=out_sem,
            recv_sem=in_sem,
            device_id=ids(*peer),
            device_id_type=MESH,
        )

    lines = []
    for d in range(1, 4):
        for p, (first, wide) in enumerate(CUTS):
            peer = line_at(p, 4 - d, *me)
            for n, (src, dst) in enumerate(
                (
                    (table.at[p, d], tables.at[p, d]),
                    (rows.at[:, pl.ds(first, wide)], held[p].at[d]),
                )
            ):
                copy = remote(src, dst, line_out.at[n, p, d - 1], line_in.at[n, p, d - 1], peer)
                copy.start()
                lines.append(copy)
    for copy in lines:
        copy.wait_recv()

    lane = lax.broadcasted_iota(jnp.int32, (16, 4 * ROWS), 1) // ROWS
    line = lax.broadcasted_iota(jnp.int32, (16, 4 * ROWS), 0)
    aim = jnp.where(lane == line // 4, line % 4, -100).astype(f32)

    def wide_table(p, n):
        t = jnp.concatenate([tables[p, d, n].astype(f32) for d in range(4)], axis=1)
        return jnp.broadcast_to(t[:, None, :], (PLANE, 16, 4 * ROWS))

    def hot(p, k):
        return wide_table(p, 0) == (aim + 4.0 * k.astype(f32))[None]

    def spread(way, k, src, dst):
        def one(n, _):
            i = n * 11 % PLANE
            for p in range(3):
                remote(
                    src[p].at[k, i],
                    dst[p].at[k, opposite(i)],
                    plane_out.at[way, k, p],
                    plane_in.at[way, k, p],
                    plane_at(p, i, *me),
                ).start()
            return 0

        lax.fori_loop(1, PLANE, one, 0)

    def all_of(way, k, src, dst, p):
        most = pl.ds(1, PLANE - 1)
        return remote(
            src[p].at[k, most],
            dst[p].at[k, most],
            plane_out.at[way, k, p],
            plane_in.at[way, k, p],
            plane_at(p, 1, *me),
        )

    def dispatch(k, _):
        for p, (first, wide) in enumerate(CUTS):
            picks = jnp.where(hot(p, k), 1.0, 0.0).astype(bf16).reshape(ROUND_ROWS, 4 * ROWS)
            o = jnp.dot(
                picks, held[p][...].reshape(4 * ROWS, wide), preferred_element_type=f32
            ).astype(bf16)
            went[p][k] = o.reshape(PLANE, 16, wide)
            came[p][k, 0] = o[:16]
        spread(0, k, went, came)
        return 0

    lax.fori_loop(0, ROUNDS, dispatch, 0)
    for load in loads:
        load.wait()

    def expert(k, _):
        for p, (first, wide) in enumerate(CUTS):
            all_of(0, k, went, came, p).wait_recv()
            part = came[p][k].reshape(ROUND_ROWS, wide)
            if p:
                part = jnp.dot(reorder(p, False), part, preferred_element_type=f32).astype(bf16)
            x_rows[:, first : first + wide] = part
        x = x_rows[...]
        gate = jnp.dot(x, wg[...], preferred_element_type=f32)
        up = jnp.dot(x, wu[...], preferred_element_type=f32)
        hidden = (gate / (1.0 + jnp.exp(-gate)) * up).astype(bf16)
        y_rows[...] = jnp.dot(hidden, wd[...], preferred_element_type=f32).astype(bf16)
        for p, (first, wide) in enumerate(CUTS):
            part = y_rows[:, first : first + wide]
            if p:
                part = jnp.dot(reorder(p, True), part, preferred_element_type=f32).astype(bf16)
            all_of(0, k, went, came, p).wait_send()
            went[p][k] = part.reshape(PLANE, 16, wide)
            back[p][k, 0] = part[:16]
        spread(1, k, went, back)
        return 0

    lax.fori_loop(0, ROUNDS, expert, 0)

    for p in range(3):
        sums[p][...] = jnp.zeros_like(sums[p])

    def combine(k, _):
        for p, (first, wide) in enumerate(CUTS):
            weights = jnp.where(hot(p, k), wide_table(p, 1), 0.0)
            weights = weights.astype(bf16).reshape(ROUND_ROWS, 4 * ROWS)
            all_of(1, k, went, back, p).wait_recv()
            sums[p][...] += lax.dot_general(
                weights,
                back[p][k].reshape(ROUND_ROWS, wide),
                (((0,), (0,)), ((), ())),
                preferred_element_type=f32,
            )
        return 0

    lax.fori_loop(0, ROUNDS, combine, 0)
    ends = []
    for p in range(3):
        for d in range(1, 4):
            gave[p][d - 1] = sums[p][d * ROWS : (d + 1) * ROWS, :].astype(bf16)
            copy = remote(
                gave[p].at[d - 1],
                got[p].at[d - 1],
                line_out.at[2, p, d - 1],
                line_in.at[2, p, d - 1],
                line_at(p, d, *me),
            )
            copy.start()
            ends.append(copy)
    for p, (first, wide) in enumerate(CUTS):
        total = sums[p][:ROWS, :]
        for d in range(3):
            ends[3 * p + d].wait_recv()
            total = total + got[p][d].astype(f32)
        out[:, first : first + wide] = (
            residual[:, first : first + wide].astype(f32) + total
        ).astype(bf16)
    for copy in lines + ends:
        copy.wait_send()

    def finish(k, _):
        for p in range(3):
            all_of(1, k, went, back, p).wait_send()
        return 0

    lax.fori_loop(0, ROUNDS, finish, 0)


def experts(table, rows, residual, w_gate, w_up, w_down):
    f32, bf16 = jnp.float32, jnp.bfloat16
    vmem = pl.BlockSpec(memory_space=pltpu.VMEM)
    apart = pl.BlockSpec(memory_space=pl.ANY)

    def parts(*front, dtype=bf16):
        return [pltpu.VMEM((*front, wide), dtype) for _, wide in CUTS]

    return pl.pallas_call(
        expert_kernel,
        out_shape=jax.ShapeDtypeStruct((ROWS, WIDTH), bf16),
        in_specs=[vmem, vmem, vmem, apart, apart, apart],
        out_specs=vmem,
        scratch_shapes=[
            pltpu.VMEM((3, 4, 2, PLANE, ROWS), bf16),
            *parts(4, ROWS),
            *parts(ROUNDS, PLANE, 16),
            *parts(ROUNDS, PLANE, 16),
            *parts(ROUNDS, PLANE, 16),
            *parts(4 * ROWS, dtype=f32),
            *parts(3, ROWS),
            *parts(3, ROWS),
            pltpu.VMEM((ROUND_ROWS, WIDTH), bf16),
            pltpu.VMEM((ROUND_ROWS, WIDTH), bf16),
            pltpu.VMEM((WIDTH, FF), bf16),
            pltpu.VMEM((WIDTH, FF), bf16),
            pltpu.VMEM((FF, WIDTH), bf16),
            pltpu.SemaphoreType.DMA((3,)),
            pltpu.SemaphoreType.DMA((3, 3, 3)),
            pltpu.SemaphoreType.DMA((3, 3, 3)),
            pltpu.SemaphoreType.DMA((2, ROUNDS, 3)),
            pltpu.SemaphoreType.DMA((2, ROUNDS, 3)),
        ],
        compiler_params=pltpu.CompilerParams(
            collective_id=1, has_side_effects=True, vmem_limit_bytes=58 << 20
        ),
    )(table, rows, residual, w_gate, w_up, w_down)


def expert_table(expert_ids, route_weights):
    f32, bf16 = jnp.float32, jnp.bfloat16
    chosen = expert_ids[:, :, None] == jnp.arange(DEVS)[None, None, :]
    counts = jnp.any(chosen, axis=1)
    before = jnp.arange(ROWS)[:, None] > jnp.arange(ROWS)[None, :]
    rank = jnp.dot(before.astype(bf16), counts.astype(bf16), preferred_element_type=f32)
    slots = jnp.where(counts, rank, -1.0)
    route = jnp.sum(
        jnp.where(chosen, (route_weights.astype(f32) / 1024.0)[:, :, None], 0.0), axis=1
    )
    i = jnp.arange(PLANE)
    wanted = []
    for p in range(3):
        for d in range(4):
            x, y, z, c = plane_at(p, i, *line_at(p, 4 - d, *place()))
            context, expert = ids(x, y, z, c)
            wanted.append(context * 8 + expert + 0 * i)
    picks = (jnp.concatenate(wanted)[:, None] == jnp.arange(DEVS)[None, :]).astype(bf16)
    table = jnp.stack(
        [
            lax.dot_general(
                picks, v.astype(bf16), (((1,), (1,)), ((), ())), preferred_element_type=f32
            )
            for v in (slots, route)
        ]
    ).astype(bf16)
    return table.reshape(2, 3, 4, PLANE, ROWS).transpose(1, 2, 0, 3, 4)


def shards(
    tokens,
    ln1_gain,
    w_query,
    key_weight,
    value_weight,
    q_gain,
    k_gain,
    w_out,
    ln2_gain,
    expert_ids,
    route_weights,
    w_gate,
    w_up,
    w_down,
):
    me = lax.axis_index("ctx") * 8 + lax.axis_index("exp")
    tables = [rope_tables(first * ROWS) for first in (me, DEVS - 1 - me)]
    cos = jnp.stack([jnp.concatenate([c, c], axis=1) for c, s in tables])
    sin = jnp.stack([jnp.concatenate([-s, s], axis=1) for c, s in tables])
    residual, normed2 = before_experts(
        tokens,
        ln1_gain.reshape(1, WIDTH),
        w_query,
        key_weight,
        value_weight,
        q_gain.reshape(1, HEAD),
        k_gain.reshape(1, HEAD),
        w_out,
        ln2_gain.reshape(1, WIDTH),
        cos,
        sin,
    )

    table = expert_table(expert_ids, route_weights)
    return experts(table, normed2, residual, w_gate[0], w_up[0], w_down[0])


def solution(mesh):
    two = P(BOTH, None)
    three = P(BOTH, None, None)
    in_specs = (
        two,
        P(),
        P(None, "exp"),
        P(),
        P(),
        P(),
        P(),
        P("exp", None),
        P(),
        two,
        two,
        three,
        three,
        three,
    )
    return jax.shard_map(shards, mesh=mesh, in_specs=in_specs, out_specs=two, check_vma=False)
```

```python
import jax
import jax.numpy as jnp
from jax import lax
from jax.experimental import pallas as pl
from jax.experimental.pallas import tpu as pltpu
from jax.sharding import PartitionSpec as P

HEAD = 128
KV_HEADS = 2
QUERY_HEADS = 16
TOP = 8
ROWS = 128
WIDTH = 2048
FF = 768
DEVS = 128
EPS = 1e-06
THETA = 1000000.0
CHUNK = 1024
BOTH = ("ctx", "exp")
MESH = pl.DeviceIdType.MESH


def rope_tables(first):
    half = HEAD // 2
    frequency = THETA ** (-2.0 * jnp.arange(half, dtype=jnp.float32) / HEAD)
    positions = (first + jnp.arange(ROWS)).astype(jnp.float32)
    angles = positions[:, None] * frequency[None, :]
    return jnp.cos(angles), jnp.sin(angles)


def place():
    c, e = lax.axis_index("ctx"), lax.axis_index("exp")
    return e // 2, (c // 2) % 2 * 2 + e % 2, c // 4, c % 2


def ids(x, y, z, core):
    return ((z * 2 + y // 2) * 2 + core, x * 2 + y % 2)


def expert_table(named, route, me):
    f32, bf16 = jnp.float32, jnp.bfloat16
    square = (DEVS, ROWS)
    expert = lax.broadcasted_iota(jnp.int32, square, 0)
    counts, weights = jnp.zeros(square, f32), jnp.zeros(square, f32)
    for k in range(TOP):
        chosen = named[k : k + 1, :] == expert
        counts = jnp.where(chosen, 1.0, counts)
        weights = jnp.where(chosen, route[k : k + 1, :].astype(f32) * (1.0 / 1024.0), weights)
    before = expert < lax.broadcasted_iota(jnp.int32, square, 1)
    rank = jnp.dot(
        counts.astype(bf16), jnp.where(before, 1.0, 0.0).astype(bf16), preferred_element_type=f32
    )
    slots = jnp.where(counts > 0.0, rank, -1.0).astype(bf16)
    shape = (PLANE, DEVS)
    i, column = lax.broadcasted_iota(jnp.int32, shape, 0), lax.broadcasted_iota(jnp.int32, shape, 1)
    picks = []
    for p in range(3):
        for d in range(4):
            context, place_in = ids(*plane_at(p, i, *line_at(p, 4 - d, *me)))
            picks.append(jnp.where(column == context * 8 + place_in, 1.0, 0.0))
    picks = jnp.concatenate(picks, axis=0).astype(bf16)
    both = [
        jnp.dot(picks, v, preferred_element_type=f32).astype(bf16)
        for v in (slots, weights.astype(bf16))
    ]
    return jnp.stack([v.reshape(12, PLANE, ROWS) for v in both], axis=1)


def norm_rows(v, gain):
    return v * lax.rsqrt(jnp.mean(v * v, axis=-1, keepdims=True) + EPS) * gain


def turn(v, cos, sin):
    return v * cos + pltpu.roll(v, HEAD // 2, 1) * sin


def layer_kernel(
    tokens,
    ln1,
    far_query,
    far_key,
    far_value,
    q_gain,
    k_gain,
    far_out,
    ln2,
    cos,
    sin,
    named,
    route,
    residual,
    normed2,
    table,
    w_query,
    w_key,
    w_value,
    w_out,
    normed,
    own,
    buf,
    wq,
    wo,
    qe,
    acc,
    top,
    attended,
    leaving,
    landing,
    kept,
    load_sem,
    out_sem,
    in_sem,
):
    f32, bf16 = jnp.float32, jnp.bfloat16
    x, y, z, c = place()
    yh, yl = y // 2, y % 2
    b = lax.axis_index("ctx") * 8 + lax.axis_index("exp")
    x1, y1 = x + 1 - 2 * (x % 2), y + 1 - 2 * (y % 2)
    near = [(lax.rem(x + dx, 4), lax.rem(c + dc, 2)) for dc in range(2) for dx in range(4)]
    ys = [lax.rem(y + d, 4) for d in range(1, 4)]
    zs = [lax.rem(z + d, 4) for d in range(1, 4)]
    other = ids(x, y, z, 1 - c)
    partner = ids(3 - x, 3 - y, 3 - z, 1 - c)
    beside, along, diagonal = ids(x, y1, z, c), ids(x1, y, z, c), ids(x1, y1, z, c)

    barrier = pltpu.get_barrier_semaphore()
    peers = [ids(px, y, z, pc) for px, pc in near[1:]]
    peers += [ids(x, py, z, c) for py in ys] + [ids(x, y, pz, c) for pz in zs]
    peers += [partner, diagonal]
    for peer in peers:
        pl.semaphore_signal(barrier, inc=1, device_id=peer, device_id_type=MESH)

    pairs = ((far_key, w_key), (far_value, w_value), (far_query, w_query), (far_out, w_out))
    loads = [
        pltpu.make_async_copy(src, dst, load_sem.at[n]) for n, (src, dst) in enumerate(pairs)
    ]
    for load in loads:
        load.start()
    sent = []

    def send(src, dst, peer):
        copy = pltpu.make_async_remote_copy(
            src_ref=src,
            dst_ref=dst,
            send_sem=out_sem.at[len(sent)],
            recv_sem=in_sem.at[len(sent)],
            device_id=peer,
            device_id_type=MESH,
        )
        copy.start()
        sent.append(copy)
        return copy

    rows = norm_rows(tokens[...].astype(f32), ln1[...]).astype(bf16)
    normed[0] = rows
    pl.semaphore_wait(barrier, len(peers))
    half = far_query.at[:, pl.ds(pl.multiple_of(c * HEAD, HEAD), HEAD)]
    q1 = send(half, wq.at[0, c], beside)
    q2 = send(half, wq.at[1, c], along)
    swap = send(normed.at[0], normed.at[1], partner)
    loads[0].wait()
    loads[1].wait()
    keys = jnp.dot(rows, w_key[...], preferred_element_type=f32)
    values = jnp.dot(rows, w_value[...], preferred_element_type=f32).astype(bf16)
    for g in range(KV_HEADS):
        k = norm_rows(keys[:, g * HEAD : (g + 1) * HEAD], k_gain[...])
        own[g, 0] = turn(k, cos[0], sin[0]).astype(bf16)
        own[g, 1] = values[:, g * HEAD : (g + 1) * HEAD]
    buf[c, z, yh, c, x, yl] = own[x // 2, c]
    first = []
    for px, pc in near[1:]:
        first.append(
            send(own.at[px // 2, pc], buf.at[pc, z, yh, c, x, yl], ids(px, y, z, pc))
        )
    table[...] = expert_table(named[...], route[...], (x, y, z, c)).reshape(table.shape)
    for copy in first:
        copy.wait_recv()

    low, high = pl.ds(0, 2), pl.ds(2, 2)
    two, four = pl.ds(0, 2), pl.ds(0, 4)
    a1 = buf.at[c, z, yh, two, low, yl]
    b1 = buf.at[c, z, yh, two, high, yl]
    second = [send(a1, a1, ids(x, py, z, c)) for py in ys]
    second += [send(b1, b1, ids(x, y, pz, c)) for pz in zs]
    for copy in second:
        copy.wait_recv()

    def of_z(pz, part=two):
        return buf.at[c, pz, part, two, low, two]

    def of_y(py, part=four):
        return buf.at[c, part, py // 2, two, high, py % 2]

    up_z, down_z, up_y, down_y = zs[0], zs[2], ys[0], ys[2]
    third = [
        send(of_z(z), of_z(z), ids(x, y, up_z, c)),
        send(of_z(z), of_z(z), ids(x, y, down_z, c)),
        send(of_y(y), of_y(y), ids(x, up_y, z, c)),
        send(of_y(y), of_y(y), ids(x, down_y, z, c)),
    ]
    handed = [send(of_z(z), of_z(z), other), send(of_y(y), of_y(y), other)]
    q1.wait_recv()
    q3 = send(wq.at[0, c], wq.at[2, c], along)
    handed_q = [send(wq.at[0, c], wq.at[0, c], other)]
    q2.wait_recv()
    handed_q.append(send(wq.at[1, c], wq.at[1, c], other))

    third[0].wait_recv()
    part = of_z(down_z, pl.ds(0, 1))
    fourth = [send(part, part, ids(x, y, up_z, c))]
    handed.append(send(of_z(down_z), of_z(down_z), other))
    third[1].wait_recv()
    part = of_z(up_z, pl.ds(1, 1))
    fourth.append(send(part, part, ids(x, y, down_z, c)))
    handed.append(send(of_z(up_z), of_z(up_z), other))
    third[2].wait_recv()
    part = of_y(down_y, pl.ds(0, 2))
    fourth.append(send(part, part, ids(x, up_y, z, c)))
    handed.append(send(of_y(down_y), of_y(down_y), other))
    third[3].wait_recv()
    part = of_y(up_y, pl.ds(2, 2))
    fourth.append(send(part, part, ids(x, down_y, z, c)))
    handed.append(send(of_y(up_y), of_y(up_y), other))

    scale = HEAD ** (-0.5) * 1.4426950408889634

    def queries(index, weights):
        both = jnp.dot(
            normed[...].reshape(2 * ROWS, WIDTH), weights, preferred_element_type=f32
        )
        for h in range(2):
            for p in range(2):
                v = both[p * ROWS : (p + 1) * ROWS, h * HEAD : (h + 1) * HEAD]
                v = turn(norm_rows(v, q_gain[...]), cos[p], sin[p]).astype(bf16)
                v = v.astype(f32) * scale
                v_hi = v.astype(bf16)
                here = pl.ds((index * 2 + h) * ROWS, ROWS)
                qe[p, here, :HEAD] = v_hi
                qe[p, here, HEAD:] = (v - v_hi.astype(f32)).astype(bf16)

    out_half = far_out.at[pl.ds(pl.multiple_of(c * HEAD, HEAD), HEAD), :]
    o1 = send(out_half, wo.at[0, c], beside)
    o2 = send(out_half, wo.at[1, c], along)
    loads[2].wait()
    loads[3].wait()
    swap.wait_recv()
    queries(0, w_query[...])
    q3.wait_recv()
    handed_q.append(send(wq.at[2, c], wq.at[2, c], other))
    for t in range(3):
        handed_q[t].wait_recv()
        queries(t + 1, jnp.concatenate([wq[t, 0], wq[t, 1]], axis=1))

    heads = QUERY_HEADS // KV_HEADS
    tall = heads * ROWS
    sub = 256
    acc[...] = jnp.zeros_like(acc)
    top[...] = jnp.full_like(top, -1e30)

    def step(p, block, jz, jy, high_half, base, masked):
        part = pl.ds(2 * high_half, 2)
        k = buf[0, jz, jy, :, part].reshape(CHUNK, HEAD)
        v = buf[1, jz, jy, :, part].reshape(CHUNK, HEAD)
        ke = jnp.concatenate([k, k], axis=1)
        ve = jnp.concatenate([v, jnp.ones_like(v)], axis=1)
        scores = [
            lax.dot_general(
                qe[p, pl.ds(r * sub, sub), :],
                ke,
                (((1,), (1,)), ((), ())),
                preferred_element_type=f32,
            )
            for r in range(tall // sub)
        ]
        for r, s in enumerate(scores):
            here = pl.ds(r * sub, sub)
            if masked:
                row = lax.broadcasted_iota(jnp.int32, s.shape, 0) % ROWS + block * ROWS
                col = lax.broadcasted_iota(jnp.int32, s.shape, 1)
                col = col + col // (CHUNK // 2) * (CHUNK // 2) + base * ROWS
                s = jnp.where(col <= row, s, -1e30)
            old = top[p, here, :]
            new = jnp.maximum(old, jnp.max(s, axis=1, keepdims=True))
            top[p, here, :] = new
            weights = jnp.exp2(s - new[:, :1]).astype(bf16)
            fade = jnp.exp2(old - new)
            o = jnp.dot(weights, ve, preferred_element_type=f32)
            acc[p, here, :] = acc[p, here, :] * jnp.concatenate([fade, fade], axis=1) + o

    def chunks(first_chunk, last_chunk, find):
        def body(n, _):
            p = n % 2
            jz, jy, high_half = find(n // 2)
            block = b + p * (DEVS - 1 - 2 * b)
            base = (jz * 2 + jy) * 16 + high_half * 4

            @pl.when(base + 11 < block)
            def _():
                step(p, block, jz, jy, high_half, base, False)

            @pl.when((base <= block) & (base + 11 >= block))
            def _():
                step(p, block, jz, jy, high_half, base, True)

            return 0

        lax.fori_loop(2 * first_chunk, 2 * last_chunk, body, 0)

    def early(m):
        late = m // 6
        jz = (1 - late) * ((z + 3 + m // 2) % 4) + late * (m - 6)
        return jz, (1 - late) * (m % 2) + late * yh, late

    def later(m):
        late = (m + 4) // 6
        return (1 - late) * ((z + 2) % 4) + late * (m - 2), (1 - late) * m + late * (1 - yh), late

    for copy in handed[:6]:
        copy.wait_recv()
    chunks(0, 5, early)
    fourth[0].wait_recv()
    far = lax.rem(z + 2, 4)
    handed.append(send(of_z(far, pl.ds(0, 1)), of_z(far, pl.ds(0, 1)), other))
    fourth[1].wait_recv()
    handed.append(send(of_z(far, pl.ds(1, 1)), of_z(far, pl.ds(1, 1)), other))
    fourth[2].wait_recv()
    far = lax.rem(y + 2, 4)
    handed.append(send(of_y(far, pl.ds(0, 2)), of_y(far, pl.ds(0, 2)), other))
    fourth[3].wait_recv()
    handed.append(send(of_y(far, pl.ds(2, 2)), of_y(far, pl.ds(2, 2)), other))
    o1.wait_recv()
    o3 = send(wo.at[0, c], wo.at[2, c], along)
    handed_o = [send(wo.at[0, c], wo.at[0, c], other)]
    chunks(5, 10, early)
    o2.wait_recv()
    handed_o.append(send(wo.at[1, c], wo.at[1, c], other))
    for copy in handed[6:]:
        copy.wait_recv()
    chunks(0, 6, later)
    for p in range(2):
        for h in range(heads):
            here = pl.ds(h * ROWS, ROWS)
            attended[p * ROWS : (p + 1) * ROWS, h * HEAD : (h + 1) * HEAD] = (
                acc[p, here, :HEAD] / acc[p, here, HEAD:]
            ).astype(bf16)
    o3.wait_recv()
    handed_o.append(send(wo.at[2, c], wo.at[2, c], other))
    for copy in handed_o:
        copy.wait_recv()
    back = []
    wide = 512
    for n in range(WIDTH // wide):
        here = pl.ds(n * wide, wide)
        o = jnp.dot(attended[:, : 2 * HEAD], w_out[:, here], preferred_element_type=f32)
        for t in range(3):
            o = o + jnp.dot(
                attended[:, (t + 1) * 2 * HEAD : (t + 2) * 2 * HEAD],
                wo[t, :, :, here].reshape(2 * HEAD, wide),
                preferred_element_type=f32,
            )
        leaving[n] = o[ROWS:].astype(bf16)
        kept[:, here] = o[:ROWS]
        back.append(send(leaving.at[n], landing.at[n], partner))
    total = jnp.zeros((ROWS, 1), f32)
    for n in range(WIDTH // wide):
        here = pl.ds(n * wide, wide)
        back[n].wait_recv()
        r = tokens[:, here].astype(f32) + (kept[:, here] + landing[n].astype(f32))
        r = r.astype(bf16)
        residual[:, here] = r
        r = r.astype(f32)
        total = total + jnp.sum(r * r, axis=-1, keepdims=True)
    r = residual[...].astype(f32)
    normed2[...] = (r * lax.rsqrt(total * (1.0 / WIDTH) + EPS) * ln2[...]).astype(bf16)
    for copy in sent:
        copy.wait_send()


def before_experts(*args):
    f32, bf16 = jnp.float32, jnp.bfloat16
    vmem = pl.BlockSpec(memory_space=pltpu.VMEM)
    apart = pl.BlockSpec(memory_space=pl.ANY)
    rows = QUERY_HEADS // KV_HEADS * ROWS
    made = jax.ShapeDtypeStruct((ROWS, WIDTH), bf16)
    copies = 64
    return pl.pallas_call(
        layer_kernel,
        out_shape=(made, made, jax.ShapeDtypeStruct((3, 4, 2, PLANE, ROWS), bf16)),
        in_specs=[apart if n in (2, 3, 4, 7) else vmem for n in range(len(args))],
        out_specs=(vmem, vmem, vmem),
        scratch_shapes=[
            pltpu.VMEM((WIDTH, 2 * HEAD), bf16),
            pltpu.VMEM((WIDTH, 2 * HEAD), bf16),
            pltpu.VMEM((WIDTH, 2 * HEAD), bf16),
            pltpu.VMEM((2 * HEAD, WIDTH), bf16),
            pltpu.VMEM((2, ROWS, WIDTH), bf16),
            pltpu.VMEM((KV_HEADS, 2, ROWS, HEAD), bf16),
            pltpu.VMEM((2, 4, 2, 2, 4, 2, ROWS, HEAD), bf16),
            pltpu.VMEM((3, 2, WIDTH, HEAD), bf16),
            pltpu.VMEM((3, 2, HEAD, WIDTH), bf16),
            pltpu.VMEM((2, rows, 2 * HEAD), bf16),
            pltpu.VMEM((2, rows, 2 * HEAD), f32),
            pltpu.VMEM((2, rows, HEAD), f32),
            pltpu.VMEM((2 * ROWS, rows), bf16),
            pltpu.VMEM((4, ROWS, 512), bf16),
            pltpu.VMEM((4, ROWS, 512), bf16),
            pltpu.VMEM((ROWS, WIDTH), f32),
            pltpu.SemaphoreType.DMA((4,)),
            pltpu.SemaphoreType.DMA((copies,)),
            pltpu.SemaphoreType.DMA((copies,)),
        ],
        compiler_params=pltpu.CompilerParams(
            collective_id=0, has_side_effects=True, vmem_limit_bytes=60 << 20
        ),
    )(*args)


CUTS = ((0, 768), (768, 640), (1408, 640))
ROUNDS = 3
PLANE = 32
ROUND_ROWS = 512


def line_at(p, d, x, y, z, c):
    if p == 0:
        return x, y, (z + d) % 4, c
    if p == 1:
        return x, (y + d) % 4, z, c
    return (x + d) % 4, y, z, c


def plane_at(p, i, x, y, z, c):
    a, b, dc = i % 4, i // 4 % 4, i // 16
    if p == 0:
        return (x + a) % 4, (y + b) % 4, z, (c + dc) % 2
    if p == 1:
        return (x + b) % 4, y, (z + a) % 4, (c + dc) % 2
    return x, (y + a) % 4, (z + b) % 4, (c + dc) % 2


def opposite(i):
    return (4 - i % 4) % 4 + (4 - i // 4 % 4) % 4 * 4 + i // 16 * 16


def reorder(p, turned):
    shape = (ROUND_ROWS, ROUND_ROWS)
    r = lax.broadcasted_iota(jnp.int32, shape, 1 if turned else 0)
    j = lax.broadcasted_iota(jnp.int32, shape, 0 if turned else 1)
    dz, dx, dy = r // 4 % 4, r // 16 % 4, r // 64 % 4
    inner, low, high = (dy, dz, dx) if p == 1 else (dx, dy, dz)
    same = j == r // 256 * 256 + high * 64 + low * 16 + inner * 4 + r % 4
    return jnp.where(same, 1.0, 0.0).astype(jnp.bfloat16)


def expert_kernel(
    table,
    rows,
    w_gate,
    w_up,
    w_down,
    out,
    tables,
    held0,
    held1,
    held2,
    went0,
    went1,
    went2,
    came0,
    came1,
    came2,
    back0,
    back1,
    back2,
    sums0,
    sums1,
    sums2,
    gave0,
    gave1,
    gave2,
    got0,
    got1,
    got2,
    x_rows,
    y_rows,
    wg,
    wu,
    wd,
    w_sem,
    line_out,
    line_in,
    plane_out,
    plane_in,
):
    f32, bf16 = jnp.float32, jnp.bfloat16
    me = place()
    held, went, came = (held0, held1, held2), (went0, went1, went2), (came0, came1, came2)
    back, sums = (back0, back1, back2), (sums0, sums1, sums2)
    gave, got = (gave0, gave1, gave2), (got0, got1, got2)

    barrier = pltpu.get_barrier_semaphore()

    def greet(i, _):
        for p in range(3):
            pl.semaphore_signal(
                barrier, inc=1, device_id=ids(*plane_at(p, i, *me)), device_id_type=MESH
            )
        return 0

    lax.fori_loop(1, PLANE, greet, 0)
    loads = [
        pltpu.make_async_copy(src, dst, w_sem.at[n])
        for n, (src, dst) in enumerate(((w_gate, wg), (w_up, wu), (w_down, wd)))
    ]
    for p, (first, wide) in enumerate(CUTS):
        loads.append(
            pltpu.make_async_copy(
                rows.at[:, pl.ds(first, wide)], held[p].at[0], w_sem.at[3 + 2 * p]
            )
        )
        loads.append(pltpu.make_async_copy(table.at[p, 0], tables.at[p, 0], w_sem.at[4 + 2 * p]))
    for load in loads[3:]:
        load.start()
    pl.semaphore_wait(barrier, 3 * (PLANE - 1))

    def remote(src, dst, out_sem, in_sem, peer):
        return pltpu.make_async_remote_copy(
            src_ref=src,
            dst_ref=dst,
            send_sem=out_sem,
            recv_sem=in_sem,
            device_id=ids(*peer),
            device_id_type=MESH,
        )

    lines = []
    for d in range(1, 4):
        for p, (first, wide) in enumerate(CUTS):
            peer = line_at(p, 4 - d, *me)
            for n, (src, dst) in enumerate(
                (
                    (table.at[p, d], tables.at[p, d]),
                    (rows.at[:, pl.ds(first, wide)], held[p].at[d]),
                )
            ):
                copy = remote(src, dst, line_out.at[n, p, d - 1], line_in.at[n, p, d - 1], peer)
                copy.start()
                lines.append(copy)
    for load in loads[:3]:
        load.start()
    for load in loads[3:]:
        load.wait()
    for copy in lines:
        copy.wait_recv()

    lane = lax.broadcasted_iota(jnp.int32, (16, 4 * ROWS), 1) // ROWS
    line = lax.broadcasted_iota(jnp.int32, (16, 4 * ROWS), 0)
    aim = jnp.where(lane == line // 4, line % 4, -100).astype(f32)

    def wide_table(p, n):
        t = jnp.concatenate([tables[p, d, n].astype(f32) for d in range(4)], axis=1)
        return jnp.broadcast_to(t[:, None, :], (PLANE, 16, 4 * ROWS))

    def hot(p, k):
        return wide_table(p, 0) == (aim + 4.0 * k.astype(f32))[None]

    def spread(way, k, src, dst, which):
        def one(n, _):
            i = n * 11 % PLANE
            for p in which:
                remote(
                    src[p].at[k, i],
                    dst[p].at[k, opposite(i)],
                    plane_out.at[way, k, p],
                    plane_in.at[way, k, p],
                    plane_at(p, i, *me),
                ).start()
            return 0

        lax.fori_loop(1, PLANE, one, 0)

    def all_of(way, k, src, dst, p):
        most = pl.ds(1, PLANE - 1)
        return remote(
            src[p].at[k, most],
            dst[p].at[k, most],
            plane_out.at[way, k, p],
            plane_in.at[way, k, p],
            plane_at(p, 1, *me),
        )

    def dispatch(k, _):
        for p, (first, wide) in enumerate(CUTS):
            picks = jnp.where(hot(p, k), 1.0, 0.0).astype(bf16).reshape(ROUND_ROWS, 4 * ROWS)
            o = jnp.dot(
                picks, held[p][...].reshape(4 * ROWS, wide), preferred_element_type=f32
            ).astype(bf16)
            went[p][k] = o.reshape(PLANE, 16, wide)
            came[p][k, 0] = o[:16]
            spread(0, k, went, came, (p,))
        return 0

    lax.fori_loop(0, ROUNDS, dispatch, 0)
    for load in loads[:3]:
        load.wait()

    def expert(k, _):
        for p, (first, wide) in enumerate(CUTS):
            all_of(0, k, went, came, p).wait_recv()
            part = came[p][k].reshape(ROUND_ROWS, wide)
            if p:
                part = jnp.dot(reorder(p, False), part, preferred_element_type=f32).astype(bf16)
            x_rows[:, first : first + wide] = part
        x = x_rows[...]
        gate = jnp.dot(x, wg[...], preferred_element_type=f32)
        up = jnp.dot(x, wu[...], preferred_element_type=f32)
        hidden = (gate / (1.0 + jnp.exp(-gate)) * up).astype(bf16)
        y_rows[...] = jnp.dot(hidden, wd[...], preferred_element_type=f32).astype(bf16)
        for p, (first, wide) in enumerate(CUTS):
            part = y_rows[:, first : first + wide]
            if p:
                part = jnp.dot(reorder(p, True), part, preferred_element_type=f32).astype(bf16)
            all_of(0, k, went, came, p).wait_send()
            went[p][k] = part.reshape(PLANE, 16, wide)
            back[p][k, 0] = part[:16]
        spread(1, k, went, back, (0, 1, 2))
        return 0

    lax.fori_loop(0, ROUNDS, expert, 0)

    for p in range(3):
        sums[p][...] = jnp.zeros_like(sums[p])

    def combine(p, k):
        weights = jnp.where(hot(p, k), wide_table(p, 1), 0.0)
        weights = weights.astype(bf16).reshape(ROUND_ROWS, 4 * ROWS)
        all_of(1, k, went, back, p).wait_recv()
        sums[p][...] += lax.dot_general(
            weights,
            back[p][k].reshape(ROUND_ROWS, CUTS[p][1]),
            (((0,), (0,)), ((), ())),
            preferred_element_type=f32,
        )

    def add_up(k, _):
        for p in range(3):
            combine(p, k)
        return 0

    lax.fori_loop(0, ROUNDS - 1, add_up, 0)
    ends = []
    for p in range(3):
        combine(p, jnp.int32(ROUNDS - 1))
        for d in range(1, 4):
            gave[p][d - 1] = sums[p][d * ROWS : (d + 1) * ROWS, :].astype(bf16)
            copy = remote(
                gave[p].at[d - 1],
                got[p].at[d - 1],
                line_out.at[2, p, d - 1],
                line_in.at[2, p, d - 1],
                line_at(p, d, *me),
            )
            copy.start()
            ends.append(copy)
    for p, (first, wide) in enumerate(CUTS):
        total = sums[p][:ROWS, :]
        for d in range(3):
            ends[3 * p + d].wait_recv()
            total = total + got[p][d].astype(f32)
        out[:, first : first + wide] = total
    for copy in lines + ends:
        copy.wait_send()

    def finish(k, _):
        for p in range(3):
            all_of(1, k, went, back, p).wait_send()
        return 0

    lax.fori_loop(0, ROUNDS, finish, 0)


def experts(table, rows, w_gate, w_up, w_down):
    f32, bf16 = jnp.float32, jnp.bfloat16
    vmem = pl.BlockSpec(memory_space=pltpu.VMEM)
    apart = pl.BlockSpec(memory_space=pl.ANY)

    def parts(*front, dtype=bf16):
        return [pltpu.VMEM((*front, wide), dtype) for _, wide in CUTS]

    return pl.pallas_call(
        expert_kernel,
        out_shape=jax.ShapeDtypeStruct((ROWS, WIDTH), f32),
        in_specs=[apart] * 5,
        out_specs=vmem,
        scratch_shapes=[
            pltpu.VMEM((3, 4, 2, PLANE, ROWS), bf16),
            *parts(4, ROWS),
            *parts(ROUNDS, PLANE, 16),
            *parts(ROUNDS, PLANE, 16),
            *parts(ROUNDS, PLANE, 16),
            *parts(4 * ROWS, dtype=f32),
            *parts(3, ROWS),
            *parts(3, ROWS),
            pltpu.VMEM((ROUND_ROWS, WIDTH), bf16),
            pltpu.VMEM((ROUND_ROWS, WIDTH), bf16),
            pltpu.VMEM((WIDTH, FF), bf16),
            pltpu.VMEM((WIDTH, FF), bf16),
            pltpu.VMEM((FF, WIDTH), bf16),
            pltpu.SemaphoreType.DMA((9,)),
            pltpu.SemaphoreType.DMA((3, 3, 3)),
            pltpu.SemaphoreType.DMA((3, 3, 3)),
            pltpu.SemaphoreType.DMA((2, ROUNDS, 3)),
            pltpu.SemaphoreType.DMA((2, ROUNDS, 3)),
        ],
        compiler_params=pltpu.CompilerParams(
            collective_id=1, has_side_effects=True, vmem_limit_bytes=60 << 20
        ),
    )(table, rows, w_gate, w_up, w_down)


def shards(
    tokens,
    ln1_gain,
    w_query,
    key_weight,
    value_weight,
    q_gain,
    k_gain,
    w_out,
    ln2_gain,
    expert_ids,
    route_weights,
    w_gate,
    w_up,
    w_down,
):
    me = lax.axis_index("ctx") * 8 + lax.axis_index("exp")
    tables = [rope_tables(first * ROWS) for first in (me, DEVS - 1 - me)]
    cos = jnp.stack([jnp.concatenate([c, c], axis=1) for c, s in tables])
    sin = jnp.stack([jnp.concatenate([-s, s], axis=1) for c, s in tables])
    residual, normed2, table = before_experts(
        tokens,
        ln1_gain.reshape(1, WIDTH),
        w_query,
        key_weight,
        value_weight,
        q_gain.reshape(1, HEAD),
        k_gain.reshape(1, HEAD),
        w_out,
        ln2_gain.reshape(1, WIDTH),
        cos,
        sin,
        expert_ids.T,
        route_weights.T,
    )
    mixture = experts(table, normed2, w_gate[0], w_up[0], w_down[0])
    return (residual.astype(jnp.float32) + mixture).astype(jnp.bfloat16)


def solution(mesh):
    two = P(BOTH, None)
    three = P(BOTH, None, None)
    in_specs = (
        two,
        P(),
        P(None, "exp"),
        P(),
        P(),
        P(),
        P(),
        P("exp", None),
        P(),
        two,
        two,
        three,
        three,
        three,
    )
    return jax.shard_map(shards, mesh=mesh, in_specs=in_specs, out_specs=two, check_vma=False)
```

```python
import jax
import jax.numpy as jnp
from jax import lax
from jax.experimental import pallas as pl
from jax.experimental.pallas import tpu as pltpu
from jax.sharding import PartitionSpec as P

HEAD = 128
KV_HEADS = 2
QUERY_HEADS = 16
TOP = 8
ROWS = 128
WIDTH = 2048
FF = 768
DEVS = 128
EPS = 1e-06
THETA = 1000000.0
CHUNK = 1024
BOTH = ("ctx", "exp")
MESH = pl.DeviceIdType.MESH


def rope_tables(first):
    half = HEAD // 2
    frequency = THETA ** (-2.0 * jnp.arange(half, dtype=jnp.float32) / HEAD)
    positions = (first + jnp.arange(ROWS)).astype(jnp.float32)
    angles = positions[:, None] * frequency[None, :]
    return jnp.cos(angles), jnp.sin(angles)


def place():
    c, e = lax.axis_index("ctx"), lax.axis_index("exp")
    return e // 2, (c // 2) % 2 * 2 + e % 2, c // 4, c % 2


def ids(x, y, z, core):
    return ((z * 2 + y // 2) * 2 + core, x * 2 + y % 2)


def expert_table(named, route, me):
    f32, bf16 = jnp.float32, jnp.bfloat16
    square = (DEVS, ROWS)
    expert = lax.broadcasted_iota(jnp.int32, square, 0)
    counts, weights = jnp.zeros(square, f32), jnp.zeros(square, f32)
    for k in range(TOP):
        chosen = named[k : k + 1, :] == expert
        counts = jnp.where(chosen, 1.0, counts)
        weights = jnp.where(chosen, route[k : k + 1, :].astype(f32) * (1.0 / 1024.0), weights)
    before = expert < lax.broadcasted_iota(jnp.int32, square, 1)
    rank = jnp.dot(
        counts.astype(bf16), jnp.where(before, 1.0, 0.0).astype(bf16), preferred_element_type=f32
    )
    slots = jnp.where(counts > 0.0, rank, -1.0).astype(bf16)
    shape = (PLANE, DEVS)
    i, column = lax.broadcasted_iota(jnp.int32, shape, 0), lax.broadcasted_iota(jnp.int32, shape, 1)
    picks = []
    for p in range(3):
        for d in range(4):
            context, place_in = ids(*plane_at(p, i, *line_at(p, 4 - d, *me)))
            picks.append(jnp.where(column == context * 8 + place_in, 1.0, 0.0))
    picks = jnp.concatenate(picks, axis=0).astype(bf16)
    both = [
        jnp.dot(picks, v, preferred_element_type=f32).astype(bf16)
        for v in (slots, weights.astype(bf16))
    ]
    return jnp.stack([v.reshape(12, PLANE, ROWS) for v in both], axis=1)


def norm_rows(v, gain):
    return v * lax.rsqrt(jnp.mean(v * v, axis=-1, keepdims=True) + EPS) * gain


def turn(v, cos, sin):
    return v * cos + pltpu.roll(v, HEAD // 2, 1) * sin


def layer_kernel(
    tokens,
    ln1,
    far_query,
    far_key,
    far_value,
    q_gain,
    k_gain,
    far_out,
    ln2,
    cos,
    sin,
    named,
    route,
    residual,
    normed2,
    table,
    w_query,
    w_key,
    w_value,
    w_out,
    normed,
    own,
    buf,
    wq,
    wo,
    qe,
    acc,
    top,
    attended,
    leaving,
    landing,
    kept,
    load_sem,
    out_sem,
    in_sem,
):
    f32, bf16 = jnp.float32, jnp.bfloat16
    x, y, z, c = place()
    yh, yl = y // 2, y % 2
    b = lax.axis_index("ctx") * 8 + lax.axis_index("exp")
    x1, y1 = x + 1 - 2 * (x % 2), y + 1 - 2 * (y % 2)
    near = [(lax.rem(x + dx, 4), lax.rem(c + dc, 2)) for dc in range(2) for dx in range(4)]
    ys = [lax.rem(y + d, 4) for d in range(1, 4)]
    zs = [lax.rem(z + d, 4) for d in range(1, 4)]
    other = ids(x, y, z, 1 - c)
    partner = ids(3 - x, 3 - y, 3 - z, 1 - c)
    beside, along, diagonal = ids(x, y1, z, c), ids(x1, y, z, c), ids(x1, y1, z, c)

    barrier = pltpu.get_barrier_semaphore()
    peers = [ids(px, y, z, pc) for px, pc in near[1:]]
    peers += [ids(x, py, z, c) for py in ys] + [ids(x, y, pz, c) for pz in zs]
    peers += [partner, diagonal]
    for peer in peers:
        pl.semaphore_signal(barrier, inc=1, device_id=peer, device_id_type=MESH)

    pairs = ((far_key, w_key), (far_value, w_value), (far_query, w_query), (far_out, w_out))
    loads = [
        pltpu.make_async_copy(src, dst, load_sem.at[n]) for n, (src, dst) in enumerate(pairs)
    ]
    for load in loads:
        load.start()
    sent = []

    def send(src, dst, peer):
        copy = pltpu.make_async_remote_copy(
            src_ref=src,
            dst_ref=dst,
            send_sem=out_sem.at[len(sent)],
            recv_sem=in_sem.at[len(sent)],
            device_id=peer,
            device_id_type=MESH,
        )
        copy.start()
        sent.append(copy)
        return copy

    rows = norm_rows(tokens[...].astype(f32), ln1[...]).astype(bf16)
    normed[0] = rows
    pl.semaphore_wait(barrier, len(peers))
    half = far_query.at[:, pl.ds(pl.multiple_of(c * HEAD, HEAD), HEAD)]
    q1 = send(half, wq.at[0, c], beside)
    q2 = send(half, wq.at[1, c], along)
    swap = send(normed.at[0], normed.at[1], partner)
    loads[0].wait()
    loads[1].wait()
    keys = jnp.dot(rows, w_key[...], preferred_element_type=f32)
    values = jnp.dot(rows, w_value[...], preferred_element_type=f32).astype(bf16)
    for g in range(KV_HEADS):
        k = norm_rows(keys[:, g * HEAD : (g + 1) * HEAD], k_gain[...])
        own[g, 0] = turn(k, cos[0], sin[0]).astype(bf16)
        own[g, 1] = values[:, g * HEAD : (g + 1) * HEAD]
    buf[c, z, yh, c, x, yl] = own[x // 2, c]
    first = []
    for px, pc in near[1:]:
        first.append(
            send(own.at[px // 2, pc], buf.at[pc, z, yh, c, x, yl], ids(px, y, z, pc))
        )
    table[...] = expert_table(named[...], route[...], (x, y, z, c)).reshape(table.shape)
    for copy in first:
        copy.wait_recv()

    low, high = pl.ds(0, 2), pl.ds(2, 2)
    two, four = pl.ds(0, 2), pl.ds(0, 4)
    a1 = buf.at[c, z, yh, two, low, yl]
    b1 = buf.at[c, z, yh, two, high, yl]
    second = [send(a1, a1, ids(x, py, z, c)) for py in ys]
    second += [send(b1, b1, ids(x, y, pz, c)) for pz in zs]
    for copy in second:
        copy.wait_recv()

    def of_z(pz, part=two):
        return buf.at[c, pz, part, two, low, two]

    def of_y(py, part=four):
        return buf.at[c, part, py // 2, two, high, py % 2]

    up_z, down_z, up_y, down_y = zs[0], zs[2], ys[0], ys[2]
    third = [
        send(of_z(z), of_z(z), ids(x, y, up_z, c)),
        send(of_z(z), of_z(z), ids(x, y, down_z, c)),
        send(of_y(y), of_y(y), ids(x, up_y, z, c)),
        send(of_y(y), of_y(y), ids(x, down_y, z, c)),
    ]
    handed = [send(of_z(z), of_z(z), other), send(of_y(y), of_y(y), other)]
    q1.wait_recv()
    q3 = send(wq.at[0, c], wq.at[2, c], along)
    handed_q = [send(wq.at[0, c], wq.at[0, c], other)]
    q2.wait_recv()
    handed_q.append(send(wq.at[1, c], wq.at[1, c], other))

    third[0].wait_recv()
    part = of_z(down_z, pl.ds(0, 1))
    fourth = [send(part, part, ids(x, y, up_z, c))]
    handed.append(send(of_z(down_z), of_z(down_z), other))
    third[1].wait_recv()
    part = of_z(up_z, pl.ds(1, 1))
    fourth.append(send(part, part, ids(x, y, down_z, c)))
    handed.append(send(of_z(up_z), of_z(up_z), other))
    third[2].wait_recv()
    part = of_y(down_y, pl.ds(0, 2))
    fourth.append(send(part, part, ids(x, up_y, z, c)))
    handed.append(send(of_y(down_y), of_y(down_y), other))
    third[3].wait_recv()
    part = of_y(up_y, pl.ds(2, 2))
    fourth.append(send(part, part, ids(x, down_y, z, c)))
    handed.append(send(of_y(up_y), of_y(up_y), other))

    scale = HEAD ** (-0.5) * 1.4426950408889634

    def queries(index, weights):
        both = jnp.dot(
            normed[...].reshape(2 * ROWS, WIDTH), weights, preferred_element_type=f32
        )
        for h in range(2):
            for p in range(2):
                v = both[p * ROWS : (p + 1) * ROWS, h * HEAD : (h + 1) * HEAD]
                v = turn(norm_rows(v, q_gain[...]), cos[p], sin[p]).astype(bf16)
                v = v.astype(f32) * scale
                v_hi = v.astype(bf16)
                here = pl.ds((index * 2 + h) * ROWS, ROWS)
                qe[p, here, :HEAD] = v_hi
                qe[p, here, HEAD:] = (v - v_hi.astype(f32)).astype(bf16)

    out_half = far_out.at[pl.ds(pl.multiple_of(c * HEAD, HEAD), HEAD), :]
    o1 = send(out_half, wo.at[0, c], beside)
    o2 = send(out_half, wo.at[1, c], along)
    loads[2].wait()
    loads[3].wait()
    swap.wait_recv()
    queries(0, w_query[...])
    q3.wait_recv()
    handed_q.append(send(wq.at[2, c], wq.at[2, c], other))
    for t in range(3):
        handed_q[t].wait_recv()
        queries(t + 1, jnp.concatenate([wq[t, 0], wq[t, 1]], axis=1))

    heads = QUERY_HEADS // KV_HEADS
    tall = heads * ROWS
    sub = 256
    acc[...] = jnp.zeros_like(acc)
    top[...] = jnp.full_like(top, -1e30)

    def step(p, block, places, base, masked):
        k, v = (
            jnp.concatenate(
                [
                    buf[n, jz, jy, :, pl.ds(2 * high_half, 2)].reshape(CHUNK, HEAD)
                    for jz, jy, high_half in places
                ],
                axis=0,
            )
            for n in range(2)
        )
        ke = jnp.concatenate([k, k], axis=1)
        ve = jnp.concatenate([v, jnp.ones_like(v)], axis=1)
        scores = [
            lax.dot_general(
                qe[p, pl.ds(r * sub, sub), :],
                ke,
                (((1,), (1,)), ((), ())),
                preferred_element_type=f32,
            )
            for r in range(tall // sub)
        ]
        for r, s in enumerate(scores):
            here = pl.ds(r * sub, sub)
            if masked:
                row = lax.broadcasted_iota(jnp.int32, s.shape, 0) % ROWS + block * ROWS
                col = lax.broadcasted_iota(jnp.int32, s.shape, 1)
                col = col + col // (CHUNK // 2) * (CHUNK // 2) + base * ROWS
                s = jnp.where(col <= row, s, -1e30)
            old = top[p, here, :]
            new = jnp.maximum(old, jnp.max(s, axis=1, keepdims=True))
            top[p, here, :] = new
            weights = jnp.exp2(s - new[:, :1]).astype(bf16)
            fade = jnp.exp2(old - new)
            o = jnp.dot(weights, ve, preferred_element_type=f32)
            acc[p, here, :] = acc[p, here, :] * jnp.concatenate([fade, fade], axis=1) + o

    def chunks(first_chunk, last_chunk, find):
        def body(n, _):
            p = n % 2
            block = b + p * (DEVS - 1 - 2 * b)
            places = [find(n // 2 * 2), find(n // 2 * 2 + 1)]
            bases = [(jz * 2 + jy) * 16 + high_half * 4 for jz, jy, high_half in places]
            whole = (bases[0] + 11 < block) & (bases[1] + 11 < block)

            @pl.when(whole)
            def _():
                step(p, block, places, 0, False)

            def one(m, _):
                place_m = find(n // 2 * 2 + m)
                base = (place_m[0] * 2 + place_m[1]) * 16 + place_m[2] * 4

                @pl.when(base + 11 < block)
                def _():
                    step(p, block, [place_m], base, False)

                @pl.when((base <= block) & (base + 11 >= block))
                def _():
                    step(p, block, [place_m], base, True)

                return 0

            @pl.when(jnp.logical_not(whole))
            def _():
                lax.fori_loop(0, 2, one, 0)

            return 0

        lax.fori_loop(first_chunk, last_chunk, body, 0)

    def early(m):
        late = m // 6
        jz = (1 - late) * ((z + 3 + m // 2) % 4) + late * (m - 6)
        return jz, (1 - late) * (m % 2) + late * yh, late

    def later(m):
        late = (m + 4) // 6
        return (1 - late) * ((z + 2) % 4) + late * (m - 2), (1 - late) * m + late * (1 - yh), late

    for copy in handed[:6]:
        copy.wait_recv()
    chunks(0, 4, early)
    fourth[0].wait_recv()
    far = lax.rem(z + 2, 4)
    handed.append(send(of_z(far, pl.ds(0, 1)), of_z(far, pl.ds(0, 1)), other))
    fourth[1].wait_recv()
    handed.append(send(of_z(far, pl.ds(1, 1)), of_z(far, pl.ds(1, 1)), other))
    fourth[2].wait_recv()
    far = lax.rem(y + 2, 4)
    handed.append(send(of_y(far, pl.ds(0, 2)), of_y(far, pl.ds(0, 2)), other))
    fourth[3].wait_recv()
    handed.append(send(of_y(far, pl.ds(2, 2)), of_y(far, pl.ds(2, 2)), other))
    o1.wait_recv()
    o3 = send(wo.at[0, c], wo.at[2, c], along)
    handed_o = [send(wo.at[0, c], wo.at[0, c], other)]
    chunks(4, 10, early)
    o2.wait_recv()
    handed_o.append(send(wo.at[1, c], wo.at[1, c], other))
    for copy in handed[6:]:
        copy.wait_recv()
    chunks(0, 6, later)
    for p in range(2):
        for h in range(heads):
            here = pl.ds(h * ROWS, ROWS)
            attended[p * ROWS : (p + 1) * ROWS, h * HEAD : (h + 1) * HEAD] = (
                acc[p, here, :HEAD] / acc[p, here, HEAD:]
            ).astype(bf16)
    o3.wait_recv()
    handed_o.append(send(wo.at[2, c], wo.at[2, c], other))
    for copy in handed_o:
        copy.wait_recv()
    back = []
    wide = 512
    for n in range(WIDTH // wide):
        here = pl.ds(n * wide, wide)
        o = jnp.dot(attended[:, : 2 * HEAD], w_out[:, here], preferred_element_type=f32)
        for t in range(3):
            o = o + jnp.dot(
                attended[:, (t + 1) * 2 * HEAD : (t + 2) * 2 * HEAD],
                wo[t, :, :, here].reshape(2 * HEAD, wide),
                preferred_element_type=f32,
            )
        leaving[n] = o[ROWS:].astype(bf16)
        kept[:, here] = o[:ROWS]
        back.append(send(leaving.at[n], landing.at[n], partner))
    total = jnp.zeros((ROWS, 1), f32)
    for n in range(WIDTH // wide):
        here = pl.ds(n * wide, wide)
        back[n].wait_recv()
        r = tokens[:, here].astype(f32) + (kept[:, here] + landing[n].astype(f32))
        r = r.astype(bf16)
        residual[:, here] = r
        r = r.astype(f32)
        total = total + jnp.sum(r * r, axis=-1, keepdims=True)
    r = residual[...].astype(f32)
    normed2[...] = (r * lax.rsqrt(total * (1.0 / WIDTH) + EPS) * ln2[...]).astype(bf16)
    for copy in sent:
        copy.wait_send()


def before_experts(*args):
    f32, bf16 = jnp.float32, jnp.bfloat16
    vmem = pl.BlockSpec(memory_space=pltpu.VMEM)
    apart = pl.BlockSpec(memory_space=pl.ANY)
    rows = QUERY_HEADS // KV_HEADS * ROWS
    made = jax.ShapeDtypeStruct((ROWS, WIDTH), bf16)
    copies = 64
    return pl.pallas_call(
        layer_kernel,
        out_shape=(made, made, jax.ShapeDtypeStruct((3, 4, 2, PLANE, ROWS), bf16)),
        in_specs=[apart if n in (2, 3, 4, 7) else vmem for n in range(len(args))],
        out_specs=(vmem, vmem, vmem),
        scratch_shapes=[
            pltpu.VMEM((WIDTH, 2 * HEAD), bf16),
            pltpu.VMEM((WIDTH, 2 * HEAD), bf16),
            pltpu.VMEM((WIDTH, 2 * HEAD), bf16),
            pltpu.VMEM((2 * HEAD, WIDTH), bf16),
            pltpu.VMEM((2, ROWS, WIDTH), bf16),
            pltpu.VMEM((KV_HEADS, 2, ROWS, HEAD), bf16),
            pltpu.VMEM((2, 4, 2, 2, 4, 2, ROWS, HEAD), bf16),
            pltpu.VMEM((3, 2, WIDTH, HEAD), bf16),
            pltpu.VMEM((3, 2, HEAD, WIDTH), bf16),
            pltpu.VMEM((2, rows, 2 * HEAD), bf16),
            pltpu.VMEM((2, rows, 2 * HEAD), f32),
            pltpu.VMEM((2, rows, HEAD), f32),
            pltpu.VMEM((2 * ROWS, rows), bf16),
            pltpu.VMEM((4, ROWS, 512), bf16),
            pltpu.VMEM((4, ROWS, 512), bf16),
            pltpu.VMEM((ROWS, WIDTH), f32),
            pltpu.SemaphoreType.DMA((4,)),
            pltpu.SemaphoreType.DMA((copies,)),
            pltpu.SemaphoreType.DMA((copies,)),
        ],
        compiler_params=pltpu.CompilerParams(
            collective_id=0, has_side_effects=True, vmem_limit_bytes=60 << 20
        ),
    )(*args)


CUTS = ((0, 768), (768, 640), (1408, 640))
ROUNDS = 3
PLANE = 32
ROUND_ROWS = 512


def line_at(p, d, x, y, z, c):
    if p == 0:
        return x, y, (z + d) % 4, c
    if p == 1:
        return x, (y + d) % 4, z, c
    return (x + d) % 4, y, z, c


def plane_at(p, i, x, y, z, c):
    a, b, dc = i % 4, i // 4 % 4, i // 16
    if p == 0:
        return (x + a) % 4, (y + b) % 4, z, (c + dc) % 2
    if p == 1:
        return (x + b) % 4, y, (z + a) % 4, (c + dc) % 2
    return x, (y + a) % 4, (z + b) % 4, (c + dc) % 2


def opposite(i):
    return (4 - i % 4) % 4 + (4 - i // 4 % 4) % 4 * 4 + i // 16 * 16


def reorder(p, turned):
    shape = (ROUND_ROWS, ROUND_ROWS)
    r = lax.broadcasted_iota(jnp.int32, shape, 1 if turned else 0)
    j = lax.broadcasted_iota(jnp.int32, shape, 0 if turned else 1)
    dz, dx, dy = r // 4 % 4, r // 16 % 4, r // 64 % 4
    inner, low, high = (dy, dz, dx) if p == 1 else (dx, dy, dz)
    same = j == r // 256 * 256 + high * 64 + low * 16 + inner * 4 + r % 4
    return jnp.where(same, 1.0, 0.0).astype(jnp.bfloat16)


def expert_kernel(
    table,
    rows,
    w_gate,
    w_up,
    w_down,
    out,
    tables,
    held0,
    held1,
    held2,
    went0,
    went1,
    went2,
    came0,
    came1,
    came2,
    back0,
    back1,
    back2,
    sums0,
    sums1,
    sums2,
    gave0,
    gave1,
    gave2,
    got0,
    got1,
    got2,
    x_rows,
    y_rows,
    wg,
    wu,
    wd,
    w_sem,
    line_out,
    line_in,
    plane_out,
    plane_in,
):
    f32, bf16 = jnp.float32, jnp.bfloat16
    me = place()
    held, went, came = (held0, held1, held2), (went0, went1, went2), (came0, came1, came2)
    back, sums = (back0, back1, back2), (sums0, sums1, sums2)
    gave, got = (gave0, gave1, gave2), (got0, got1, got2)

    barrier = pltpu.get_barrier_semaphore()

    def greet(i, _):
        for p in range(3):
            pl.semaphore_signal(
                barrier, inc=1, device_id=ids(*plane_at(p, i, *me)), device_id_type=MESH
            )
        return 0

    lax.fori_loop(1, PLANE, greet, 0)
    loads = [
        pltpu.make_async_copy(src, dst, w_sem.at[n])
        for n, (src, dst) in enumerate(((w_gate, wg), (w_up, wu), (w_down, wd)))
    ]
    for p, (first, wide) in enumerate(CUTS):
        loads.append(
            pltpu.make_async_copy(
                rows.at[:, pl.ds(first, wide)], held[p].at[0], w_sem.at[3 + 2 * p]
            )
        )
        loads.append(pltpu.make_async_copy(table.at[p, 0], tables.at[p, 0], w_sem.at[4 + 2 * p]))
    for load in loads[3:]:
        load.start()
    pl.semaphore_wait(barrier, 3 * (PLANE - 1))

    def remote(src, dst, out_sem, in_sem, peer):
        return pltpu.make_async_remote_copy(
            src_ref=src,
            dst_ref=dst,
            send_sem=out_sem,
            recv_sem=in_sem,
            device_id=ids(*peer),
            device_id_type=MESH,
        )

    lines = []
    for d in range(1, 4):
        for p, (first, wide) in enumerate(CUTS):
            peer = line_at(p, 4 - d, *me)
            for n, (src, dst) in enumerate(
                (
                    (table.at[p, d], tables.at[p, d]),
                    (rows.at[:, pl.ds(first, wide)], held[p].at[d]),
                )
            ):
                copy = remote(src, dst, line_out.at[n, p, d - 1], line_in.at[n, p, d - 1], peer)
                copy.start()
                lines.append(copy)
    for load in loads[:3]:
        load.start()
    for load in loads[3:]:
        load.wait()
    for copy in lines:
        copy.wait_recv()

    lane = lax.broadcasted_iota(jnp.int32, (16, 4 * ROWS), 1) // ROWS
    line = lax.broadcasted_iota(jnp.int32, (16, 4 * ROWS), 0)
    aim = jnp.where(lane == line // 4, line % 4, -100).astype(f32)

    def wide_table(p, n):
        t = jnp.concatenate([tables[p, d, n].astype(f32) for d in range(4)], axis=1)
        return jnp.broadcast_to(t[:, None, :], (PLANE, 16, 4 * ROWS))

    def hot(p, k):
        return wide_table(p, 0) == (aim + 4.0 * k.astype(f32))[None]

    def spread(way, k, src, dst, which):
        def one(n, _):
            i = n * 11 % PLANE
            for p in which:
                remote(
                    src[p].at[k, i],
                    dst[p].at[k, opposite(i)],
                    plane_out.at[way, k, p],
                    plane_in.at[way, k, p],
                    plane_at(p, i, *me),
                ).start()
            return 0

        lax.fori_loop(1, PLANE, one, 0)

    def all_of(way, k, src, dst, p):
        most = pl.ds(1, PLANE - 1)
        return remote(
            src[p].at[k, most],
            dst[p].at[k, most],
            plane_out.at[way, k, p],
            plane_in.at[way, k, p],
            plane_at(p, 1, *me),
        )

    def dispatch(k, _):
        for p, (first, wide) in enumerate(CUTS):
            picks = jnp.where(hot(p, k), 1.0, 0.0).astype(bf16).reshape(ROUND_ROWS, 4 * ROWS)
            o = jnp.dot(
                picks, held[p][...].reshape(4 * ROWS, wide), preferred_element_type=f32
            ).astype(bf16)
            went[p][k] = o.reshape(PLANE, 16, wide)
            came[p][k, 0] = o[:16]
            spread(0, k, went, came, (p,))
        return 0

    lax.fori_loop(0, ROUNDS, dispatch, 0)
    for load in loads[:3]:
        load.wait()

    def expert(k, _):
        for p, (first, wide) in enumerate(CUTS):
            all_of(0, k, went, came, p).wait_recv()
            part = came[p][k].reshape(ROUND_ROWS, wide)
            if p:
                part = jnp.dot(reorder(p, False), part, preferred_element_type=f32).astype(bf16)
            x_rows[:, first : first + wide] = part
        x = x_rows[...]
        gate = jnp.dot(x, wg[...], preferred_element_type=f32)
        up = jnp.dot(x, wu[...], preferred_element_type=f32)
        hidden = (gate / (1.0 + jnp.exp(-gate)) * up).astype(bf16)
        y_rows[...] = jnp.dot(hidden, wd[...], preferred_element_type=f32).astype(bf16)
        for p, (first, wide) in enumerate(CUTS):
            part = y_rows[:, first : first + wide]
            if p:
                part = jnp.dot(reorder(p, True), part, preferred_element_type=f32).astype(bf16)
            all_of(0, k, went, came, p).wait_send()
            went[p][k] = part.reshape(PLANE, 16, wide)
            back[p][k, 0] = part[:16]
        spread(1, k, went, back, (0, 1, 2))
        return 0

    lax.fori_loop(0, ROUNDS, expert, 0)

    for p in range(3):
        sums[p][...] = jnp.zeros_like(sums[p])

    def combine(p, k):
        weights = jnp.where(hot(p, k), wide_table(p, 1), 0.0)
        weights = weights.astype(bf16).reshape(ROUND_ROWS, 4 * ROWS)
        all_of(1, k, went, back, p).wait_recv()
        sums[p][...] += lax.dot_general(
            weights,
            back[p][k].reshape(ROUND_ROWS, CUTS[p][1]),
            (((0,), (0,)), ((), ())),
            preferred_element_type=f32,
        )

    def add_up(k, _):
        for p in range(3):
            combine(p, k)
        return 0

    lax.fori_loop(0, ROUNDS - 1, add_up, 0)
    ends = []
    for p in range(3):
        combine(p, jnp.int32(ROUNDS - 1))
        for d in range(1, 4):
            gave[p][d - 1] = sums[p][d * ROWS : (d + 1) * ROWS, :].astype(bf16)
            copy = remote(
                gave[p].at[d - 1],
                got[p].at[d - 1],
                line_out.at[2, p, d - 1],
                line_in.at[2, p, d - 1],
                line_at(p, d, *me),
            )
            copy.start()
            ends.append(copy)
    for p, (first, wide) in enumerate(CUTS):
        total = sums[p][:ROWS, :]
        for d in range(3):
            ends[3 * p + d].wait_recv()
            total = total + got[p][d].astype(f32)
        out[:, first : first + wide] = total
    for copy in lines + ends:
        copy.wait_send()

    def finish(k, _):
        for p in range(3):
            all_of(1, k, went, back, p).wait_send()
        return 0

    lax.fori_loop(0, ROUNDS, finish, 0)


def experts(table, rows, w_gate, w_up, w_down):
    f32, bf16 = jnp.float32, jnp.bfloat16
    vmem = pl.BlockSpec(memory_space=pltpu.VMEM)
    apart = pl.BlockSpec(memory_space=pl.ANY)

    def parts(*front, dtype=bf16):
        return [pltpu.VMEM((*front, wide), dtype) for _, wide in CUTS]

    return pl.pallas_call(
        expert_kernel,
        out_shape=jax.ShapeDtypeStruct((ROWS, WIDTH), f32),
        in_specs=[apart] * 5,
        out_specs=vmem,
        scratch_shapes=[
            pltpu.VMEM((3, 4, 2, PLANE, ROWS), bf16),
            *parts(4, ROWS),
            *parts(ROUNDS, PLANE, 16),
            *parts(ROUNDS, PLANE, 16),
            *parts(ROUNDS, PLANE, 16),
            *parts(4 * ROWS, dtype=f32),
            *parts(3, ROWS),
            *parts(3, ROWS),
            pltpu.VMEM((ROUND_ROWS, WIDTH), bf16),
            pltpu.VMEM((ROUND_ROWS, WIDTH), bf16),
            pltpu.VMEM((WIDTH, FF), bf16),
            pltpu.VMEM((WIDTH, FF), bf16),
            pltpu.VMEM((FF, WIDTH), bf16),
            pltpu.SemaphoreType.DMA((9,)),
            pltpu.SemaphoreType.DMA((3, 3, 3)),
            pltpu.SemaphoreType.DMA((3, 3, 3)),
            pltpu.SemaphoreType.DMA((2, ROUNDS, 3)),
            pltpu.SemaphoreType.DMA((2, ROUNDS, 3)),
        ],
        compiler_params=pltpu.CompilerParams(
            collective_id=1, has_side_effects=True, vmem_limit_bytes=60 << 20
        ),
    )(table, rows, w_gate, w_up, w_down)


def shards(
    tokens,
    ln1_gain,
    w_query,
    key_weight,
    value_weight,
    q_gain,
    k_gain,
    w_out,
    ln2_gain,
    expert_ids,
    route_weights,
    w_gate,
    w_up,
    w_down,
):
    me = lax.axis_index("ctx") * 8 + lax.axis_index("exp")
    tables = [rope_tables(first * ROWS) for first in (me, DEVS - 1 - me)]
    cos = jnp.stack([jnp.concatenate([c, c], axis=1) for c, s in tables])
    sin = jnp.stack([jnp.concatenate([-s, s], axis=1) for c, s in tables])
    residual, normed2, table = before_experts(
        tokens,
        ln1_gain.reshape(1, WIDTH),
        w_query,
        key_weight,
        value_weight,
        q_gain.reshape(1, HEAD),
        k_gain.reshape(1, HEAD),
        w_out,
        ln2_gain.reshape(1, WIDTH),
        cos,
        sin,
        expert_ids.T,
        route_weights.T,
    )
    mixture = experts(table, normed2, w_gate[0], w_up[0], w_down[0])
    return (residual.astype(jnp.float32) + mixture).astype(jnp.bfloat16)


def solution(mesh):
    two = P(BOTH, None)
    three = P(BOTH, None, None)
    in_specs = (
        two,
        P(),
        P(None, "exp"),
        P(),
        P(),
        P(),
        P(),
        P("exp", None),
        P(),
        two,
        two,
        three,
        three,
        three,
    )
    return jax.shard_map(shards, mesh=mesh, in_specs=in_specs, out_specs=two, check_vma=False)
```
